32 devices in a mesh: section: 8 (over z, core), mp: 4 (over y, x).
Axes of the slice: x: 2, y: 2, z: 4, core: 2. Of those that a mesh axis runs over, the one named last changes fastest.
Arguments:
- matches: int32 [1024, 2], P('section'), may hold values from 0 to 7, all different within a row; in each aligned block of 128 rows (0 to 127, 128 to 255, ...) at most 64 rows name the same one
- actions: int32 [2, 1024, 2], P(None, 'section'), may hold values from 0 to 1023
- state: float32 [1024, 2, 2048], P('section', None, 'mp'), may hold values from -6 to 6
- embed: bfloat16 [1024, 2048], P(None, 'mp'), may hold values from -3 to 3
- w_in: bfloat16 [8, 1, 2048, 8192], P('section', None, None, 'mp'), may hold values from -0.125 to 0.125
- w_out: bfloat16 [8, 1, 8192, 2048], P('section', None, 'mp'), may hold values from -0.0625 to 0.0625
- head: bfloat16 [8, 2048, 1024], P('section', None, 'mp'), may hold values from -16 to 16
Outputs:
- logp: float32 [2, 1024, 2], P(None, 'section')
The draws below stay inside these ranges and needn't reach their ends.
Inputs may be any that keep to these rules, and one draw needn't show every extreme that they name: `matches`: each game names two different agents; among the 128 games of one index of section no agent is named more than 64 times, a bound that some block reaches in some of these groups.
All inputs are finite; a program needn't handle non-finite values.
Results may differ from the reference program's by a relative error of at most 0.0095.
Values may be sent and summed in bfloat16 or wider, within the bound.
No kernel may reach another device: no remote copies, remote signals or barrier semaphores. Data moves between devices by JAX's collectives and lax.ppermute only.
A program may use at most 64 MiB of HBM per device.

```python
import math
import jax
import jax.numpy as jnp
import numpy as np
from jax import lax

D = 2048
FF = 8192
ACTIONS = 1024
LAYERS = 1
STEPS = 2
GAMES_DEV = 128
AGENTS = 8
CAP = 64
SLOTS = 512
GAMES = 1024
N_MP = 4


def draw_head(key, part):
    key_base = jax.random.fold_in(key, 0)
    base = jax.random.normal(key_base, (AGENTS, D, ACTIONS), jnp.float32) * (3.0 / math.sqrt(D))
    return jnp.clip(base, -16.0, 16.0).astype(jnp.bfloat16)


def place_ends(entries, stream_key, least, high):
    dims = entries.shape
    index_at = [jax.random.randint(jax.random.fold_in(stream_key, axis), (), 0, dims[axis]) for axis in range(len(dims))]
    entries = entries.at[tuple(index_at)].set(least)
    longest = dims.index(max(dims))
    index_at[longest] = (index_at[longest] + 1) % dims[longest]
    return entries.at[tuple(index_at)].set(high)


def shard_levels(key, extent, cuts, low, high):
    loudness = 1.0
    for position, blocks in cuts:
        steps = jax.random.uniform(jax.random.fold_in(jax.random.fold_in(key, 6), position), (blocks,), jnp.float32, low / len(cuts), high / len(cuts))
        loudness = loudness * jnp.repeat(jnp.exp(steps), extent[position] // blocks).reshape((-1,) + (1,) * (len(extent) - 1 - position))
    return loudness


def deal_out(rng, own, number, rows, number_of, top, bound, skew):
    ranking = jax.random.permutation(rng, number_of)
    crowded, ordinary = load_shares(number_of, rows * top, bound, skew, True), load_shares(number_of, rows * top, bound, skew, False)
    places = jnp.arange(number_of)

    def named(lengths, turn):
        used = int((lengths > 0).sum())
        fixed = max(1, used // 4)
        shifted = fixed + (places - fixed + turn * (used - fixed)) % max(1, number_of - fixed)
        return jnp.zeros((number_of,), jnp.int32).at[ranking[jnp.where(places < fixed, places, shifted)]].set(jnp.asarray(lengths, jnp.int32))

    lengths = jnp.where(number % 4 == 0, named(crowded, number // 4), named(ordinary, number - number // 4 - 1))
    mixed = jax.random.permutation(jax.random.fold_in(own, 3), number_of)
    source_of, sink = mixed[0:number_of // 2 * 2:2], mixed[1:number_of // 2 * 2:2]
    slack = jnp.minimum(lengths[source_of] - 1, bound - lengths[sink]) // 2
    slack = jnp.where((source_of == ranking[0]) | (sink == ranking[0]) | (lengths[sink] == 0), 0, jnp.maximum(slack, 0))
    shifted = jax.random.randint(jax.random.fold_in(own, 4), (number_of // 2,), 0, 1 << 20) % (slack + 1)
    lengths = lengths.at[source_of].add(-shifted).at[sink].add(shifted)
    labels = jnp.searchsorted(jnp.cumsum(lengths), jnp.arange(rows * top), side="right").astype(jnp.int32)
    table = labels.reshape(top, rows).T
    table = table[jax.random.permutation(jax.random.fold_in(own, 1), rows)]
    turn = jax.random.randint(jax.random.fold_in(own, 2), (rows, 1), 0, top)
    return jnp.take_along_axis(table, (jnp.arange(top)[None, :] + turn) % top, axis=1)


def load_shares(amount, total, bound, lean, full):
    loads = [(1 << 20) // math.isqrt(grade ** lean) + 1 for grade in range(1, amount + 1)]
    largest = bound if full else min(bound, max(-(-total // amount), total * loads[0] // sum(loads)))
    least = 1 if total - largest >= amount - 1 else 0
    given, rest = [largest] + [least] * (amount - 1), total - largest - least * (amount - 1)
    while rest > 0:
        free = [i for i in range(1, amount) if given[i] < largest] or [i for i in range(1, amount) if given[i] < bound]
        mass, budget = sum([loads[i] for i in free]), rest
        for i in free:
            extra = min(bound - given[i], max(1, budget * loads[i] // mass), rest)
            given[i] = given[i] + extra
            rest = rest - extra
    return np.array(given)


def centred(own_key, shape, width, bound, cuts=(), kind=jnp.bfloat16):
    array = jax.random.normal(own_key, shape, jnp.float32) * width
    if len(cuts) > 0:
        array = shard_levels(own_key, shape, cuts, -0.22, 0.18) * array
    return jnp.clip(array, min=-bound, max=bound).astype(kind)


def setup_inputs(seed: int = 0) -> dict:
    seeds = jax.random.split(jax.random.key(seed), 8)
    matches_keys = jax.random.split(jax.random.fold_in(seeds[0], 1), GAMES // GAMES_DEV)
    matches_turns = jax.random.permutation(jax.random.fold_in(seeds[0], 3), GAMES // GAMES_DEV)
    matches = jax.vmap(lambda own, number: deal_out(jax.random.fold_in(seeds[0], 2), own, number, GAMES_DEV, AGENTS, 2, CAP, 2))(matches_keys, matches_turns).reshape((GAMES, 2))
    actions = place_ends(jax.random.randint(seeds[1], (STEPS, GAMES, 2), 0, ACTIONS), jax.random.fold_in(seeds[1], 1), 0, ACTIONS - 1).astype(jnp.int32)
    state = centred(seeds[2], (GAMES, 2, D), 1.0, 6.0, ((0, 8), (2, 4)), jnp.float32)
    embed = centred(seeds[3], (ACTIONS, D), 0.5, 3.0, ((1, 4),))
    w_in = centred(seeds[4], (AGENTS, LAYERS, D, FF), D ** -0.5, 0.125, ((0, 8), (3, 4)))
    w_out = centred(seeds[5], (AGENTS, LAYERS, FF, D), FF ** -0.5, 0.0625, ((0, 8), (2, 4)))
    head = draw_head(jax.random.fold_in(seeds[7], 71), 0)
    return {"matches": matches, "actions": actions, "state": state, "embed": embed, "w_in": w_in, "w_out": w_out, "head": head}


norm_eps = 1e-06

def rms_round(source):
    widened = source.astype(jnp.float32)
    scale = lax.rsqrt(lax.optimization_barrier(jnp.mean(widened * widened, axis=-1, keepdims=True)) + norm_eps)
    return (widened * scale).astype(jnp.bfloat16)

def agent_logits(row_block, in_weights, out_weights, head_weights):
    layer_in = row_block
    summed = row_block.astype(jnp.float32)
    for layer_idx in range(LAYERS):
        normed = rms_round(layer_in)
        hidden = jax.nn.gelu(jnp.dot(normed, in_weights[layer_idx], preferred_element_type=jnp.float32)).astype(jnp.bfloat16)
        groups = hidden.astype(jnp.float32).reshape(hidden.shape[0], N_MP, FF // N_MP)
        blocks = out_weights[layer_idx].astype(jnp.float32).reshape(N_MP, FF // N_MP, D)
        partial_value = jnp.einsum('bmf,mfd->bmd', groups, blocks).astype(jnp.bfloat16)
        partial_value = lax.optimization_barrier(partial_value).astype(jnp.float32)
        summed = layer_in.astype(jnp.float32) + lax.optimization_barrier(jnp.sum(partial_value, axis=1))
        if layer_idx + 1 < LAYERS:
            layer_in = summed.astype(jnp.bfloat16)
    return jnp.dot(rms_round(summed), head_weights, preferred_element_type=jnp.float32)

def reference(matches, actions, state, embed, w_in, w_out, head):
    owners = matches.reshape(-1).astype(jnp.int32)
    total_rows = owners.shape[0]
    row_order = jnp.argsort(owners, stable=True).astype(jnp.int32)
    counts = lax.optimization_barrier(jnp.sum((owners[:, None] == jnp.arange(AGENTS, dtype=jnp.int32)[None, :]).astype(jnp.int32), axis=0))
    starts = (jnp.cumsum(counts) - counts).astype(jnp.int32)
    padded_order = jnp.concatenate([row_order, jnp.zeros((SLOTS,), jnp.int32)])
    current = state
    results = []
    for step_idx in range(STEPS):
        rows_all = current.reshape(total_rows, D).astype(jnp.bfloat16)
        chosen = actions[step_idx].reshape(-1).astype(jnp.int32)

        def serve_agent(packed):
            agent_id, in_weights, out_weights, head_weights = packed
            row_index = lax.dynamic_slice(padded_order, (starts[agent_id],), (SLOTS,)).astype(jnp.int32)
            is_live = jnp.arange(SLOTS, dtype=jnp.int32) < counts[agent_id]
            logits = agent_logits(rows_all[row_index], in_weights, out_weights, head_weights)
            row_peak = lax.optimization_barrier(jnp.max(logits, axis=1, keepdims=True))
            row_total = lax.optimization_barrier(jnp.sum(jnp.exp(logits - row_peak), axis=1))
            picked = jnp.take_along_axis(logits, chosen[row_index][:, None], axis=1)[:, 0]
            row_value = picked - row_peak[:, 0] - jnp.log(row_total)
            return (jnp.where(is_live, row_value, 0.0), jnp.where(is_live, row_index, total_rows))
        row_values, targets = lax.map(serve_agent, (jnp.arange(AGENTS, dtype=jnp.int32), w_in, w_out, head))
        logp = jnp.zeros((total_rows + 1,), jnp.float32).at[targets.reshape(-1)].add(row_values.reshape(-1))[:total_rows]
        results.append(logp.reshape(GAMES, 2))
        picked_rows = jnp.take(embed, actions[step_idx], axis=0).astype(jnp.float32)
        current = 0.8 * current + picked_rows + 0.5 * picked_rows[:, ::-1, :]
    return jnp.stack(results)
```

```python
import functools

import jax
import jax.numpy as jnp
from jax import lax
from jax.experimental import pallas as pl
from jax.experimental.pallas import tpu as pltpu
from jax.sharding import PartitionSpec as P

STEPS = 2
META = 8
DIGIT = 32
VMEM = 48 * 1024 * 1024

norm_eps = 1e-06
f32 = jnp.float32
bf16 = jnp.bfloat16


def rms_round(source):
    widened = source.astype(f32)
    scale = lax.rsqrt(jnp.mean(widened * widened, axis=-1, keepdims=True) + norm_eps)
    return (widened * scale).astype(bf16)


def iota(shape, dim):
    return lax.broadcasted_iota(jnp.int32, shape, dim)


def nt_dot(left, right):
    return lax.dot_general(left, right, (((1,), (1,)), ((), ())), preferred_element_type=f32)


def slots_row(own_row, own_col):
    rows = own_row.shape[1]
    earlier = (own_col == own_row) & (iota((rows, rows), 0) < iota((rows, rows), 1))
    return jnp.sum(earlier.astype(jnp.int32), axis=0, keepdims=True)


def pack_kernel(sections, cap, own_row, own_col, meta, state, out):
    games, _, feat = state.shape
    rows = 2 * games
    dest = own_row[...] * cap + slots_row(own_row[...], own_col[...])
    select = (iota((sections * cap, rows), 0) == dest).astype(bf16)
    first = jnp.dot(select[:, :games], state[:, 0, :].astype(bf16), preferred_element_type=f32)
    second = jnp.dot(select[:, games:], state[:, 1, :].astype(bf16), preferred_element_type=f32)
    packed = (first + second).astype(bf16)
    notes = nt_dot(meta[...], select).astype(bf16)
    for s in range(sections):
        out[s, :cap, :] = packed[s * cap : (s + 1) * cap]
        out[s, cap:, :] = jnp.zeros((META, feat), bf16)
        out[s, cap:, :cap] = notes[:, s * cap : (s + 1) * cap]


def unpack_kernel(sections, cap, size, mp_ref, arrived, embed, x0_out, x1_out, notes_out, place_out):
    slots = sections * cap
    group = size // 4
    m = mp_ref[0]
    rows = jnp.concatenate([arrived[s, :cap, :] for s in range(sections)], axis=0)
    notes = jnp.concatenate([arrived[s, cap:, :cap] for s in range(sections)], axis=1)
    live = notes[META - 1 : META, :].astype(f32)
    before = (iota((slots, slots), 0) < iota((slots, slots), 1)).astype(bf16)
    rank = jnp.dot(jnp.broadcast_to(live, (8, slots)).astype(bf16), before, preferred_element_type=f32)
    rank = rank[:1].astype(jnp.int32)
    block = rank // group
    place = jnp.where(live > 0, (block ^ m) * group + (rank - block * group), -1)
    select = (iota((size, slots), 0) == place).astype(bf16)
    x0 = jnp.dot(select, rows, preferred_element_type=f32)
    mine = nt_dot(select, notes)
    own = (mine[:, 0:1] * DIGIT + mine[:, 1:2]).astype(jnp.int32)
    other = (mine[:, 2:3] * DIGIT + mine[:, 3:4]).astype(jnp.int32)
    columns = iota((size, embed.shape[0]), 1)
    effect = jnp.where(columns == own, 1.0, 0.0) + jnp.where(columns == other, 0.5, 0.0)
    moved = jnp.dot(effect.astype(bf16), embed[...], preferred_element_type=f32)
    x0_out[...] = x0.astype(bf16)
    x1_out[...] = (0.8 * x0 + moved).astype(bf16)
    notes_out[...] = mine[: size // 4]
    place_out[...] = place


def serve_kernel(size, tiles, mp_ref, own, px, py, da, db, w_in, w_out, send_a, send_b, keep_a, keep_b, mine, x_full, hidden, scale):
    feat = own.shape[1]
    group = size // 4
    width = w_in.shape[1]
    half = x_full.shape[1] // 2
    m = mp_ref[0]
    step = pl.program_id(0)

    @pl.when(step == 0)
    def _():
        total = jnp.zeros((size, 1), f32)
        for k in range(4):
            parts = []
            for j in range(4):
                b = j ^ k
                if k == 3:
                    src = da if b < 2 else db
                    parts.append(src[(b % 2) * group : (b % 2 + 1) * group, :])
                else:
                    src = (own, px, py)[k]
                    parts.append(src[b * group : (b + 1) * group, :])
            chunk = jnp.concatenate(parts, axis=0)
            x_full[:, pl.ds(pl.multiple_of((m ^ k) * feat, feat), feat)] = chunk
            wide = chunk.astype(f32)
            total = total + jnp.sum(wide * wide, axis=1, keepdims=True)
        scale[...] = lax.rsqrt(total / (4 * feat) + norm_eps)
        mine[...] = x_full[:group, :]

    for t in range(tiles):

        @pl.when(step == t)
        def _():
            z = jnp.dot(x_full[...], w_in[...], preferred_element_type=f32)
            hidden[:, t * width : (t + 1) * width] = jax.nn.gelu(z * scale[...]).astype(bf16)

    for t in range(tiles):

        @pl.when(step == tiles + t)
        def _():
            part = jnp.dot(hidden[...], w_out[...], preferred_element_type=f32).astype(bf16)
            g = [part[j * group : (j + 1) * group] for j in range(4)]
            if t < tiles // 2:
                cols = slice(t * width, (t + 1) * width)
                send_a[:group, cols] = g[1]
                send_a[group:, cols] = g[3]
                keep_a[:group, cols] = g[0]
                keep_a[group:, cols] = g[2]
            else:
                cols = slice(t * width - half, (t + 1) * width - half)
                send_b[:group, cols] = g[2]
                send_b[group:, cols] = g[3]
                keep_b[:group, cols] = g[0]
                keep_b[group:, cols] = g[1]


def fold_kernel(keep_a, got_a, keep_b, got_b, out_a, out_b):
    out_a[...] = (keep_a[...].astype(f32) + got_a[...].astype(f32)).astype(bf16)
    out_b[...] = (keep_b[...].astype(f32) + got_b[...].astype(f32)).astype(bf16)


def score_kernel(sections, cap, step_idx, mp_ref, mine, keep_a, got_a, last_a, keep_b, got_b, last_b, h0, h1, h2, h3a, h3b, notes, place, out):
    group, width = mine.shape
    half = width // 2
    m = mp_ref[0]
    wide = lambda ref: ref[...].astype(f32)
    sum_a = keep_a[:group].astype(f32) + got_a[:group].astype(f32) + wide(last_a)
    sum_b = keep_b[:group].astype(f32) + got_b[:group].astype(f32) + wide(last_b)
    x = wide(mine)
    ha = x[:, :half] + sum_a
    hb = x[:, half:] + sum_b
    square = jnp.sum(ha * ha, axis=1, keepdims=True) + jnp.sum(hb * hb, axis=1, keepdims=True)
    scale = lax.rsqrt(square / width + norm_eps)
    na = (ha * scale).astype(bf16)
    nb = (hb * scale).astype(bf16)
    c = 4 * step_idx
    chosen = (notes[:, c : c + 1] * DIGIT + notes[:, c + 1 : c + 2]).astype(jnp.int32)
    logits = []
    for k in range(4):
        top, bottom = (h3a[...], h3b[...]) if k == 3 else ((h0, h1, h2)[k][:half], (h0, h1, h2)[k][half:])
        logits.append(
            jnp.dot(na, top, preferred_element_type=f32) + jnp.dot(nb, bottom, preferred_element_type=f32)
        )
    peak = functools.reduce(jnp.maximum, [jnp.max(v, axis=1, keepdims=True) for v in logits])
    total = jnp.zeros((group, 1), f32)
    picked = jnp.zeros((group, 1), f32)
    for k, v in enumerate(logits):
        columns = iota(v.shape, 1) + (m ^ k) * v.shape[1]
        total = total + jnp.sum(jnp.exp(v - peak), axis=1, keepdims=True)
        picked = picked + jnp.sum(jnp.where(columns == chosen, v, 0.0), axis=1, keepdims=True)
    logp = picked - peak - jnp.log(total)
    slots = sections * cap
    spread = jnp.where(iota((group, slots), 0) == place[...], logp, 0.0)
    spread = jnp.sum(spread, axis=0, keepdims=True)
    for s in range(sections):
        out[s : s + 1, :] = spread[:, s * cap : (s + 1) * cap]


def return_kernel(sections, cap, own_row, own_col, got, out):
    rows = own_row.shape[1]
    dest = own_row[...] * cap + slots_row(own_row[...], own_col[...])
    pick = iota((sections * cap, rows), 0) == dest
    for t in range(STEPS):
        column = got[:, t : t + 1]
        out[t : t + 1, :] = jnp.sum(jnp.where(pick, column, 0.0), axis=0, keepdims=True)


def call(kernel, outs, cost=None, **kw):
    return pl.pallas_call(
        kernel,
        out_shape=outs,
        compiler_params=pltpu.CompilerParams(vmem_limit_bytes=VMEM),
        cost_estimate=cost,
        **kw,
    )


def shape(*dims, dtype=bf16):
    return jax.ShapeDtypeStruct(dims, dtype)


SMEM_SPEC = pl.BlockSpec(memory_space=pltpu.SMEM)
VMEM_SPEC = pl.BlockSpec(memory_space=pltpu.VMEM)


def plane_plan(matches, actions, state, embed, w_in, w_out, head):
    sections = lax.axis_size("section")
    games, _, feat = state.shape
    cap = 4 * games // sections
    rows = 2 * games
    slots = sections * cap
    width = 4 * feat
    m = lax.axis_index("mp").astype(jnp.int32).reshape(1)
    over_x = lambda v: lax.ppermute(v, "mp", [(i, i ^ 1) for i in range(4)])
    over_y = lambda v: lax.ppermute(v, "mp", [(i, i ^ 2) for i in range(4)])

    def gather(v):
        h = v.shape[0] // 2
        from_x, from_y = over_x(v), over_y(v)
        return from_x, from_y, over_y(from_x[:h]), over_x(from_y[h:])

    own_row = matches.T.reshape(1, rows)
    own_col = own_row.reshape(rows, 1)
    acts = actions.transpose(0, 2, 1)
    mine0, other0, mine1 = acts[0].reshape(rows), acts[0, ::-1].reshape(rows), acts[1].reshape(rows)
    notes = jnp.stack(
        [
            mine0 // DIGIT, mine0 % DIGIT, other0 // DIGIT, other0 % DIGIT,
            mine1 // DIGIT, mine1 % DIGIT, jnp.zeros_like(mine0), jnp.ones_like(mine0),
        ]
    ).astype(bf16)

    head_own = head[0]
    heads = (head_own,) + gather(head_own)

    packed = call(functools.partial(pack_kernel, sections, cap), shape(sections, cap + META, feat))(
        own_row, own_col, notes, state
    )
    arrived = lax.all_to_all(packed, "section", split_axis=0, concat_axis=0, tiled=True)
    size = slots
    group = size // 4
    x0, x1, notes_c, place = call(
        functools.partial(unpack_kernel, sections, cap, size),
        (shape(size, feat), shape(size, feat), shape(group, META, dtype=f32), shape(1, slots, dtype=jnp.int32)),
        in_specs=[SMEM_SPEC, VMEM_SPEC, VMEM_SPEC],
    )(m, arrived, embed)

    tiles = 4
    tile = w_in.shape[3] // tiles
    full = lambda r, c: pl.BlockSpec((r, c), lambda i: (0, 0))
    outs = []
    for step_idx, x in enumerate((x0, x1)):
        got = gather(x)
        send_a, send_b, keep_a, keep_b, mine = call(
            functools.partial(serve_kernel, size, tiles),
            (shape(size // 2, width // 2),) * 4 + (shape(group, width),),
            cost=pl.CostEstimate(flops=4 * size * width * w_in.shape[3], bytes_accessed=4 * width * w_in.shape[3], transcendentals=0),
            grid=(2 * tiles,),
            in_specs=[
                SMEM_SPEC,
                full(size, feat), full(size, feat), full(size, feat), full(size // 2, feat), full(size // 2, feat),
                pl.BlockSpec((w_in.shape[2], tile), lambda i: (0, jnp.minimum(i, tiles - 1))),
                pl.BlockSpec((w_out.shape[2], width // tiles), lambda i: (0, jnp.maximum(i - tiles, 0))),
            ],
            out_specs=tuple([full(size // 2, width // 2)] * 4 + [full(group, width)]),
            scratch_shapes=[
                pltpu.VMEM((size, width), bf16),
                pltpu.VMEM((size, w_in.shape[3]), bf16),
                pltpu.VMEM((size, 1), f32),
            ],
        )(m, x, *got, w_in[0, 0], w_out[0, 0])
        got_a, got_b = over_x(send_a), over_y(send_b)
        second = pl.BlockSpec((group, width // 2), lambda i: (1, 0))
        fold_a, fold_b = call(
            fold_kernel,
            (shape(group, width // 2),) * 2,
            grid=(1,),
            in_specs=[second] * 4,
            out_specs=(full(group, width // 2),) * 2,
        )(keep_a, got_a, keep_b, got_b)
        last_a, last_b = over_y(fold_a), over_x(fold_b)
        outs.append(
            call(
                functools.partial(score_kernel, sections, cap, step_idx),
                shape(sections, cap, dtype=f32),
                in_specs=[SMEM_SPEC] + [VMEM_SPEC] * 14,
            )(m, mine, keep_a, got_a, last_a, keep_b, got_b, last_b, *heads, notes_c, place)
        )
    sent = jnp.concatenate(outs, axis=1)
    sent = jnp.broadcast_to(sent[:, None], (sections, 4, STEPS * cap)).reshape(sections * 4, STEPS * cap)
    back = lax.all_to_all(sent, ("section", "mp"), split_axis=0, concat_axis=0, tiled=True)
    back = back.reshape(sections, 4, STEPS, cap).sum(axis=1)
    back = back.transpose(0, 2, 1).reshape(slots, STEPS)
    logp = call(functools.partial(return_kernel, sections, cap), shape(STEPS, rows, dtype=f32))(own_row, own_col, back)
    return logp.reshape(STEPS, 2, games).transpose(0, 2, 1)


def general_plan(matches, actions, state, embed, w_in, w_out, head):
    sections = lax.axis_size("section")
    game_count = matches.shape[0]
    feat_width = state.shape[2]
    slot_cap = 4 * game_count // sections
    served = sections * slot_cap
    owners = matches.reshape(-1)
    onehot = (owners[:, None] == jnp.arange(sections, dtype=jnp.int32)[None, :]).astype(jnp.int32)
    slot_of = jnp.sum((jnp.cumsum(onehot, axis=0) - onehot) * onehot, axis=1)
    action_width = head.shape[2]
    columns = lax.axis_index("mp") * action_width + jnp.arange(action_width, dtype=jnp.int32)
    current = state
    results = []
    for step_idx in range(STEPS):
        observed = current.astype(bf16).reshape(2 * game_count, feat_width)
        outgoing = jnp.zeros((sections, slot_cap, feat_width), bf16).at[owners, slot_of].set(observed)
        arrived = lax.all_to_all(outgoing, "section", split_axis=0, concat_axis=0, tiled=True)
        inputs = lax.all_gather(arrived.reshape(served, feat_width), "mp", axis=1, tiled=True)
        normed = rms_round(inputs)
        hidden = jax.nn.gelu(jnp.dot(normed, w_in[0, 0], preferred_element_type=f32)).astype(bf16)
        partial_value = jnp.dot(hidden, w_out[0, 0], preferred_element_type=f32)
        summed = inputs.astype(f32) + lax.psum(partial_value.astype(bf16), "mp").astype(f32)
        logits = jnp.dot(rms_round(summed), head[0], preferred_element_type=f32)
        returned = lax.all_to_all(
            logits.reshape(sections, slot_cap, action_width).astype(bf16),
            "section",
            split_axis=0,
            concat_axis=0,
            tiled=True,
        ).astype(f32)
        row_logits = returned[owners, slot_of]
        row_peak = lax.pmax(jnp.max(row_logits, axis=1), "mp")
        chosen = actions[step_idx].reshape(-1)
        local_total = jnp.sum(jnp.exp(row_logits - row_peak[:, None]), axis=1)
        local_pick = jnp.sum(jnp.where(columns[None, :] == chosen[:, None], row_logits, 0.0), axis=1)
        row_total, picked = lax.psum((local_total, local_pick), "mp")
        results.append((picked - row_peak - jnp.log(row_total)).reshape(game_count, 2))
        picked_rows = jnp.take(embed, actions[step_idx], axis=0).astype(f32)
        current = 0.8 * current + picked_rows + 0.5 * picked_rows[:, ::-1, :]
    return jnp.stack(results)


def solution(mesh):
    return jax.shard_map(
        plane_plan if mesh.shape["mp"] == 4 else general_plan,
        mesh=mesh,
        in_specs=(
            P("section", None),
            P(None, "section", None),
            P("section", None, "mp"),
            P(None, "mp"),
            P("section", None, None, "mp"),
            P("section", None, "mp", None),
            P("section", None, "mp"),
        ),
        out_specs=P(None, "section", None),
        check_vma=False,
    )
```

```python
import functools

import jax
import jax.numpy as jnp
from jax import lax
from jax.experimental import pallas as pl
from jax.experimental.pallas import tpu as pltpu
from jax.sharding import PartitionSpec as P

STEPS = 2
META = 8
DIGIT = 32
SHARES = ((1, 1), (3, 4), (1, 2))
TILE = 512
VMEM = 20 * 1024 * 1024

norm_eps = 1e-06
f32 = jnp.float32
bf16 = jnp.bfloat16


def rms_round(source):
    widened = source.astype(f32)
    scale = lax.rsqrt(jnp.mean(widened * widened, axis=-1, keepdims=True) + norm_eps)
    return (widened * scale).astype(bf16)


def iota(shape, dim):
    return lax.broadcasted_iota(jnp.int32, shape, dim)


def nt_dot(left, right):
    return lax.dot_general(left, right, (((1,), (1,)), ((), ())), preferred_element_type=f32)


def slots_row(own_row, own_col):
    rows = own_row.shape[1]
    earlier = (own_col == own_row) & (iota((rows, rows), 0) < iota((rows, rows), 1))
    return jnp.sum(earlier.astype(jnp.int32), axis=0, keepdims=True)


def pack_kernel(sections, cap, own_row, own_col, meta, state, out):
    games, _, feat = state.shape
    rows = 2 * games
    dest = own_row[...] * cap + slots_row(own_row[...], own_col[...])
    select = (iota((sections * cap, rows), 0) == dest).astype(bf16)
    first = jnp.dot(select[:, :games], state[:, 0, :].astype(bf16), preferred_element_type=f32)
    second = jnp.dot(select[:, games:], state[:, 1, :].astype(bf16), preferred_element_type=f32)
    packed = (first + second).astype(bf16)
    notes = nt_dot(meta[...], select).astype(bf16)
    for s in range(sections):
        out[s, :cap, :] = packed[s * cap : (s + 1) * cap]
        out[s, cap:, :] = jnp.zeros((META, feat), bf16)
        out[s, cap:, :cap] = notes[:, s * cap : (s + 1) * cap]


def unpack_kernel(sections, cap, mp_ref, arrived, embed, x0_out, x1_out, notes_out, place_out, count_out):
    slots = sections * cap
    m = mp_ref[0]
    rows = jnp.concatenate([arrived[s, :cap, :] for s in range(sections)], axis=0)
    notes = jnp.concatenate([arrived[s, cap:, :cap] for s in range(sections)], axis=1)
    live = notes[META - 1 : META, :].astype(f32)
    before = (iota((slots, slots), 0) < iota((slots, slots), 1)).astype(bf16)
    rank = jnp.dot(jnp.broadcast_to(live, (8, slots)).astype(bf16), before, preferred_element_type=f32)
    rank = rank[:1].astype(jnp.int32)
    served = jnp.sum(live).astype(jnp.int32)
    fits = [(served * den <= slots * num).astype(jnp.int32) for num, den in SHARES]
    count_out[0] = sum(fits[1:], 0)
    group = slots // 4
    for (num, den), fit in zip(SHARES[1:], fits[1:]):
        group = group + fit * (slots * num // den // 4 - group)
    block = sum((rank >= j * group).astype(jnp.int32) for j in range(1, 4))
    place = jnp.where(live > 0, (block ^ m) * group + (rank - block * group), -1)
    size = slots
    select = (iota((size, slots), 0) == place).astype(bf16)
    x0 = jnp.dot(select, rows, preferred_element_type=f32)
    mine = nt_dot(select, notes)
    own = (mine[:, 0:1] * DIGIT + mine[:, 1:2]).astype(jnp.int32)
    other = (mine[:, 2:3] * DIGIT + mine[:, 3:4]).astype(jnp.int32)
    columns = iota((size, embed.shape[0]), 1)
    effect = jnp.where(columns == own, 1.0, 0.0) + jnp.where(columns == other, 0.5, 0.0)
    moved = jnp.dot(effect.astype(bf16), embed[...], preferred_element_type=f32)
    x0_out[...] = x0.astype(bf16)
    x1_out[...] = (0.8 * x0 + moved).astype(bf16)
    notes_out[...] = mine[: size // 4]
    place_out[...] = place


def hidden_kernel(size, tile, mp_ref, own, px, py, da, db, w_in, hidden, mine, x_full, scale):
    feat = own.shape[1]
    group = size // 4
    width, inner = w_in.shape
    m = mp_ref[0]
    total = jnp.zeros((size, 1), f32)
    for k in range(4):
        parts = []
        for j in range(4):
            b = j ^ k
            if k == 3:
                src = da if b < 2 else db
                parts.append(src[(b % 2) * group : (b % 2 + 1) * group, :])
            else:
                src = (own, px, py)[k]
                parts.append(src[b * group : (b + 1) * group, :])
        chunk = jnp.concatenate(parts, axis=0)
        x_full[:, pl.ds(pl.multiple_of((m ^ k) * feat, feat), feat)] = chunk
        wide = chunk.astype(f32)
        total = total + jnp.sum(wide * wide, axis=1, keepdims=True)
    scale[...] = lax.rsqrt(total / width + norm_eps)
    mine[...] = x_full[:group, :]

    @pl.loop(0, inner // tile)
    def _(t):
        cols = pl.ds(pl.multiple_of(t * tile, tile), tile)
        z = jnp.dot(x_full[...], w_in[:, cols], preferred_element_type=f32)
        hidden[:, cols] = jax.nn.gelu(z * scale[...]).astype(bf16)


def part_kernel(size, tile, hidden, w_out, send_a, send_b, keep_a, keep_b):
    group = size // 4
    half = w_out.shape[1] // 2
    for side in range(2):
        keep, send, order = ((keep_a, send_a, (0, 2, 1, 3)), (keep_b, send_b, (0, 1, 2, 3)))[side]

        @pl.loop(0, half // tile)
        def _(t):
            cols = pl.ds(pl.multiple_of(t * tile, tile), tile)
            from_cols = pl.ds(pl.multiple_of(t * tile + side * half, tile), tile)
            part = jnp.dot(hidden[...], w_out[:, from_cols], preferred_element_type=f32).astype(bf16)
            for i, j in enumerate(order):
                ref = keep if i < 2 else send
                ref[(i % 2) * group : (i % 2 + 1) * group, cols] = part[j * group : (j + 1) * group]


def fold_kernel(keep_a, got_a, keep_b, got_b, out_a, out_b):
    out_a[...] = (keep_a[...].astype(f32) + got_a[...].astype(f32)).astype(bf16)
    out_b[...] = (keep_b[...].astype(f32) + got_b[...].astype(f32)).astype(bf16)


def score_kernel(sections, cap, step_idx, mp_ref, mine, keep_a, got_a, last_a, keep_b, got_b, last_b, h0, h1_top, h1_bottom, h2_top, h2_bottom, h3_top, h3_bottom, notes, place, out):
    group, width = mine.shape
    half = width // 2
    m = mp_ref[0]
    wide = lambda ref: ref[...].astype(f32)
    sum_a = keep_a[:group].astype(f32) + got_a[:group].astype(f32) + wide(last_a)
    sum_b = keep_b[:group].astype(f32) + got_b[:group].astype(f32) + wide(last_b)
    x = wide(mine)
    ha = x[:, :half] + sum_a
    hb = x[:, half:] + sum_b
    square = jnp.sum(ha * ha, axis=1, keepdims=True) + jnp.sum(hb * hb, axis=1, keepdims=True)
    scale = lax.rsqrt(square / width + norm_eps)
    na = (ha * scale).astype(bf16)
    nb = (hb * scale).astype(bf16)
    c = 4 * step_idx
    chosen = (notes[:, c : c + 1] * DIGIT + notes[:, c + 1 : c + 2]).astype(jnp.int32)
    logits = []
    heads = ((h0[:half], h0[half:]), (h1_top[...], h1_bottom[...]), (h2_top[...], h2_bottom[...]), (h3_top[...], h3_bottom[...]))
    for top, bottom in heads:
        logits.append(
            jnp.dot(na, top, preferred_element_type=f32) + jnp.dot(nb, bottom, preferred_element_type=f32)
        )
    peak = functools.reduce(jnp.maximum, [jnp.max(v, axis=1, keepdims=True) for v in logits])
    total = jnp.zeros((group, 1), f32)
    picked = jnp.zeros((group, 1), f32)
    for k, v in enumerate(logits):
        columns = iota(v.shape, 1) + (m ^ k) * v.shape[1]
        total = total + jnp.sum(jnp.exp(v - peak), axis=1, keepdims=True)
        picked = picked + jnp.sum(jnp.where(columns == chosen, v, 0.0), axis=1, keepdims=True)
    logp = picked - peak - jnp.log(total)
    slots = sections * cap
    spread = jnp.where(iota((group, slots), 0) == place[...], logp, 0.0)
    spread = jnp.sum(spread, axis=0, keepdims=True)
    for s in range(sections):
        out[s : s + 1, :] = spread[:, s * cap : (s + 1) * cap]


def return_kernel(sections, cap, own_row, own_col, got, out):
    rows = own_row.shape[1]
    dest = own_row[...] * cap + slots_row(own_row[...], own_col[...])
    pick = iota((sections * cap, rows), 0) == dest
    for t in range(STEPS):
        column = got[:, t : t + 1]
        out[t : t + 1, :] = jnp.sum(jnp.where(pick, column, 0.0), axis=0, keepdims=True)


def call(kernel, outs, cost=None, **kw):
    return pl.pallas_call(
        kernel,
        out_shape=outs,
        compiler_params=pltpu.CompilerParams(vmem_limit_bytes=VMEM),
        cost_estimate=cost,
        **kw,
    )


def shape(*dims, dtype=bf16):
    return jax.ShapeDtypeStruct(dims, dtype)


SMEM_SPEC = pl.BlockSpec(memory_space=pltpu.SMEM)
VMEM_SPEC = pl.BlockSpec(memory_space=pltpu.VMEM)


def serve_rows(sections, cap, size, over_x, over_y, m, x0, x1, notes, place, w_in, w_out, *heads):
    feat = x0.shape[1]
    width = w_in.shape[0]
    inner = w_in.shape[1]
    group = size // 4

    h = size // 2
    flops = 2 * size * width * inner

    def near(v):
        return over_x(v), over_y(v)

    def far(from_x, from_y):
        return over_y(from_x[:h]), over_x(from_y[h:])

    def to_hidden(x, near_x, far_x):
        return call(
            functools.partial(hidden_kernel, size, TILE),
            (shape(size, inner), shape(group, width)),
            cost=pl.CostEstimate(flops=flops, bytes_accessed=2 * width * inner, transcendentals=size * inner),
            in_specs=[SMEM_SPEC] + [VMEM_SPEC] * 6,
            scratch_shapes=[pltpu.VMEM((size, width), bf16), pltpu.VMEM((size, 1), f32)],
        )(m, x, *near_x, *far_x, w_in)

    def to_parts(hidden):
        return call(
            functools.partial(part_kernel, size, TILE),
            (shape(h, width // 2),) * 4,
            cost=pl.CostEstimate(flops=flops, bytes_accessed=2 * width * inner, transcendentals=0),
        )(hidden, w_out)

    def fold(keep_a, got_a, keep_b, got_b):
        second = pl.BlockSpec((group, width // 2), lambda i: (1, 0))
        whole = pl.BlockSpec((group, width // 2), lambda i: (0, 0))
        return call(
            fold_kernel,
            (shape(group, width // 2),) * 2,
            grid=(1,),
            in_specs=[second] * 4,
            out_specs=(whole,) * 2,
        )(keep_a, got_a, keep_b, got_b)

    def score(step_idx, *pieces):
        return call(
            functools.partial(score_kernel, sections, cap, step_idx),
            shape(sections, cap, dtype=f32),
            in_specs=[SMEM_SPEC] + [VMEM_SPEC] * (9 + len(heads)),
        )(m, *pieces, *heads, notes, place)

    x0, x1, notes = x0[:size], x1[:size], notes[:group]
    near0 = near(x0)
    far0 = far(*near0)
    x1, *far0 = lax.optimization_barrier((x1, *far0))
    near1 = near(x1)
    hidden0, mine0 = to_hidden(x0, near0, far0)
    hidden0, *near1 = lax.optimization_barrier((hidden0, *near1))
    far1 = far(*near1)
    send_a0, send_b0, keep_a0, keep_b0 = to_parts(hidden0)
    got_a0, got_b0 = over_x(send_a0), over_y(send_b0)
    hidden1, mine1 = to_hidden(x1, near1, far1)
    hidden1, got_a0, got_b0 = lax.optimization_barrier((hidden1, got_a0, got_b0))
    fold_a0, fold_b0 = fold(keep_a0, got_a0, keep_b0, got_b0)
    last_a0, last_b0 = over_y(fold_a0), over_x(fold_b0)
    hidden1, fold_a0 = lax.optimization_barrier((hidden1, fold_a0))
    send_a1, send_b1, keep_a1, keep_b1 = to_parts(hidden1)
    got_a1, got_b1 = over_x(send_a1), over_y(send_b1)
    fold_a1, fold_b1 = fold(keep_a1, got_a1, keep_b1, got_b1)
    last_a1, last_b1 = over_y(fold_a1), over_x(fold_b1)
    outs = (
        score(0, mine0, keep_a0, got_a0, last_a0, keep_b0, got_b0, last_b0),
        score(1, mine1, keep_a1, got_a1, last_a1, keep_b1, got_b1, last_b1),
    )
    return jnp.concatenate(outs, axis=1)


def plane_plan(matches, actions, state, embed, w_in, w_out, head):
    sections = lax.axis_size("section")
    games, _, feat = state.shape
    cap = 4 * games // sections
    rows = 2 * games
    slots = sections * cap
    width = 4 * feat
    m = lax.axis_index("mp").astype(jnp.int32).reshape(1)
    over_x = lambda v: lax.ppermute(v, "mp", [(i, i ^ 1) for i in range(4)])
    over_y = lambda v: lax.ppermute(v, "mp", [(i, i ^ 2) for i in range(4)])

    own_row = matches.T.reshape(1, rows)
    own_col = own_row.reshape(rows, 1)
    acts = actions.transpose(0, 2, 1)
    mine0, other0, mine1 = acts[0].reshape(rows), acts[0, ::-1].reshape(rows), acts[1].reshape(rows)
    notes = jnp.stack(
        [
            mine0 // DIGIT, mine0 % DIGIT, other0 // DIGIT, other0 % DIGIT,
            mine1 // DIGIT, mine1 % DIGIT, jnp.zeros_like(mine0), jnp.ones_like(mine0),
        ]
    ).astype(bf16)

    head_own = head[0]
    rows_half = head_own.shape[0] // 2
    top, bottom = head_own[:rows_half], head_own[rows_half:]
    x_top, y_bottom = over_x(top), over_y(bottom)
    others = (x_top, over_x(bottom), over_y(top), y_bottom, over_y(x_top), over_x(y_bottom))

    packed = call(functools.partial(pack_kernel, sections, cap), shape(sections, cap + META, feat))(
        own_row, own_col, notes, state
    )
    arrived = lax.all_to_all(packed, "section", split_axis=0, concat_axis=0, tiled=True)
    arrived, *others = lax.optimization_barrier((arrived,) + others)
    heads = (head_own, *others)
    x0, x1, notes_c, place, count = call(
        functools.partial(unpack_kernel, sections, cap),
        (
            shape(slots, feat), shape(slots, feat), shape(slots // 4, META, dtype=f32),
            shape(1, slots, dtype=jnp.int32), shape(1, dtype=jnp.int32),
        ),
        in_specs=[SMEM_SPEC, VMEM_SPEC, VMEM_SPEC],
        out_specs=(VMEM_SPEC,) * 4 + (SMEM_SPEC,),
    )(m, arrived, embed)

    branches = [
        functools.partial(serve_rows, sections, cap, slots * num // den, over_x, over_y) for num, den in SHARES
    ]
    sent = lax.switch(count[0], branches, m, x0, x1, notes_c, place, w_in[0, 0], w_out[0, 0], *heads)
    sent = jnp.broadcast_to(sent[:, None], (sections, 4, STEPS * cap)).reshape(sections * 4, STEPS * cap)
    back = lax.all_to_all(sent, ("section", "mp"), split_axis=0, concat_axis=0, tiled=True)
    back = back.reshape(sections, 4, STEPS, cap).sum(axis=1)
    back = back.transpose(0, 2, 1).reshape(slots, STEPS)
    logp = call(functools.partial(return_kernel, sections, cap), shape(STEPS, rows, dtype=f32))(own_row, own_col, back)
    return logp.reshape(STEPS, 2, games).transpose(0, 2, 1)


def general_plan(matches, actions, state, embed, w_in, w_out, head):
    sections = lax.axis_size("section")
    game_count = matches.shape[0]
    feat_width = state.shape[2]
    slot_cap = 4 * game_count // sections
    served = sections * slot_cap
    owners = matches.reshape(-1)
    onehot = (owners[:, None] == jnp.arange(sections, dtype=jnp.int32)[None, :]).astype(jnp.int32)
    slot_of = jnp.sum((jnp.cumsum(onehot, axis=0) - onehot) * onehot, axis=1)
    action_width = head.shape[2]
    columns = lax.axis_index("mp") * action_width + jnp.arange(action_width, dtype=jnp.int32)
    current = state
    results = []
    for step_idx in range(STEPS):
        observed = current.astype(bf16).reshape(2 * game_count, feat_width)
        outgoing = jnp.zeros((sections, slot_cap, feat_width), bf16).at[owners, slot_of].set(observed)
        arrived = lax.all_to_all(outgoing, "section", split_axis=0, concat_axis=0, tiled=True)
        inputs = lax.all_gather(arrived.reshape(served, feat_width), "mp", axis=1, tiled=True)
        normed = rms_round(inputs)
        hidden = jax.nn.gelu(jnp.dot(normed, w_in[0, 0], preferred_element_type=f32)).astype(bf16)
        partial_value = jnp.dot(hidden, w_out[0, 0], preferred_element_type=f32)
        summed = inputs.astype(f32) + lax.psum(partial_value.astype(bf16), "mp").astype(f32)
        logits = jnp.dot(rms_round(summed), head[0], preferred_element_type=f32)
        returned = lax.all_to_all(
            logits.reshape(sections, slot_cap, action_width).astype(bf16),
            "section",
            split_axis=0,
            concat_axis=0,
            tiled=True,
        ).astype(f32)
        row_logits = returned[owners, slot_of]
        row_peak = lax.pmax(jnp.max(row_logits, axis=1), "mp")
        chosen = actions[step_idx].reshape(-1)
        local_total = jnp.sum(jnp.exp(row_logits - row_peak[:, None]), axis=1)
        local_pick = jnp.sum(jnp.where(columns[None, :] == chosen[:, None], row_logits, 0.0), axis=1)
        row_total, picked = lax.psum((local_total, local_pick), "mp")
        results.append((picked - row_peak - jnp.log(row_total)).reshape(game_count, 2))
        picked_rows = jnp.take(embed, actions[step_idx], axis=0).astype(f32)
        current = 0.8 * current + picked_rows + 0.5 * picked_rows[:, ::-1, :]
    return jnp.stack(results)


def solution(mesh):
    return jax.shard_map(
        plane_plan if mesh.shape["mp"] == 4 else general_plan,
        mesh=mesh,
        in_specs=(
            P("section", None),
            P(None, "section", None),
            P("section", None, "mp"),
            P(None, "mp"),
            P("section", None, None, "mp"),
            P("section", None, "mp", None),
            P("section", None, "mp"),
        ),
        out_specs=P(None, "section", None),
        check_vma=False,
    )
```

```python
import functools

import jax
import jax.numpy as jnp
from jax import lax
from jax.experimental import pallas as pl
from jax.experimental.pallas import tpu as pltpu
from jax.sharding import PartitionSpec as P

STEPS = 2
META = 8
DIGIT = 32
SHARES = ((1, 1), (3, 4), (1, 2))
TILE = 512
VMEM = 20 * 1024 * 1024

norm_eps = 1e-06
f32 = jnp.float32
bf16 = jnp.bfloat16


def rms_round(source):
    widened = source.astype(f32)
    scale = lax.rsqrt(jnp.mean(widened * widened, axis=-1, keepdims=True) + norm_eps)
    return (widened * scale).astype(bf16)


def iota(shape, dim):
    return lax.broadcasted_iota(jnp.int32, shape, dim)


def nt_dot(left, right):
    return lax.dot_general(left, right, (((1,), (1,)), ((), ())), preferred_element_type=f32)


def slots_row(own_row, own_col):
    rows = own_row.shape[1]
    earlier = (own_col == own_row) & (iota((rows, rows), 0) < iota((rows, rows), 1))
    return jnp.sum(earlier.astype(jnp.int32), axis=0, keepdims=True)


def pack_kernel(sections, cap, own_row, own_col, meta, state, out):
    games, _, feat = state.shape
    rows = 2 * games
    dest = own_row[...] * cap + slots_row(own_row[...], own_col[...])
    select = (iota((sections * cap, rows), 0) == dest).astype(bf16)
    first = jnp.dot(select[:, :games], state[:, 0, :].astype(bf16), preferred_element_type=f32)
    second = jnp.dot(select[:, games:], state[:, 1, :].astype(bf16), preferred_element_type=f32)
    packed = (first + second).astype(bf16)
    notes = nt_dot(meta[...], select).astype(bf16)
    for s in range(sections):
        out[s, :cap, :] = packed[s * cap : (s + 1) * cap]
        out[s, cap:, :] = jnp.zeros((META, feat), bf16)
        out[s, cap:, :cap] = notes[:, s * cap : (s + 1) * cap]


def unpack_kernel(sections, cap, mp_ref, arrived, embed, x0_out, x1_out, notes_out, place_out, count_out):
    slots = sections * cap
    m = mp_ref[0]
    rows = jnp.concatenate([arrived[s, :cap, :] for s in range(sections)], axis=0)
    notes = jnp.concatenate([arrived[s, cap:, :cap] for s in range(sections)], axis=1)
    live = notes[META - 1 : META, :].astype(f32)
    before = (iota((slots, slots), 0) < iota((slots, slots), 1)).astype(bf16)
    rank = jnp.dot(jnp.broadcast_to(live, (8, slots)).astype(bf16), before, preferred_element_type=f32)
    rank = rank[:1].astype(jnp.int32)
    served = jnp.sum(live).astype(jnp.int32)
    fits = [(served * den <= slots * num).astype(jnp.int32) for num, den in SHARES]
    count_out[0] = sum(fits[1:], 0)
    group = slots // 4
    for (num, den), fit in zip(SHARES[1:], fits[1:]):
        group = group + fit * (slots * num // den // 4 - group)
    block = sum((rank >= j * group).astype(jnp.int32) for j in range(1, 4))
    place = jnp.where(live > 0, (block ^ m) * group + (rank - block * group), -1)
    size = slots
    select = (iota((size, slots), 0) == place).astype(bf16)
    x0 = jnp.dot(select, rows, preferred_element_type=f32)
    mine = nt_dot(select, notes)
    own = (mine[:, 0:1] * DIGIT + mine[:, 1:2]).astype(jnp.int32)
    other = (mine[:, 2:3] * DIGIT + mine[:, 3:4]).astype(jnp.int32)
    columns = iota((size, embed.shape[0]), 1)
    effect = jnp.where(columns == own, 1.0, 0.0) + jnp.where(columns == other, 0.5, 0.0)
    moved = jnp.dot(effect.astype(bf16), embed[...], preferred_element_type=f32)
    x0_out[...] = x0.astype(bf16)
    x1_out[...] = (0.8 * x0 + moved).astype(bf16)
    notes_out[...] = mine[: size // 4]
    place_out[...] = place


def hidden_kernel(size, tile, mp_ref, own, px, py, da, db, w_in, hidden, mine, x_full, scale):
    feat = own.shape[1]
    group = size // 4
    width, inner = w_in.shape
    m = mp_ref[0]
    total = jnp.zeros((size, 1), f32)
    for k in range(4):
        parts = []
        for j in range(4):
            b = j ^ k
            if k == 3:
                src = da if b < 2 else db
                parts.append(src[(b % 2) * group : (b % 2 + 1) * group, :])
            else:
                src = (own, px, py)[k]
                parts.append(src[b * group : (b + 1) * group, :])
        chunk = jnp.concatenate(parts, axis=0)
        x_full[:, pl.ds(pl.multiple_of((m ^ k) * feat, feat), feat)] = chunk
        wide = chunk.astype(f32)
        total = total + jnp.sum(wide * wide, axis=1, keepdims=True)
    scale[...] = lax.rsqrt(total / width + norm_eps)
    mine[...] = x_full[:group, :]

    @pl.loop(0, inner // tile)
    def _(t):
        cols = pl.ds(pl.multiple_of(t * tile, tile), tile)
        z = jnp.dot(x_full[...], w_in[:, cols], preferred_element_type=f32)
        hidden[:, cols] = jax.nn.gelu(z * scale[...]).astype(bf16)


def near_kernel(size, tile, mp_ref, own, px, py, w_in, z, square, chunks, w_here, arrived):
    feat = own.shape[1]
    group = size // 4
    m = mp_ref[0]

    def fetch(k, t):
        rows = pl.ds(pl.multiple_of((m ^ k) * feat, feat), feat)
        cols = pl.ds(pl.multiple_of(t * tile, tile), tile)
        return pltpu.make_async_copy(w_in.at[rows, cols], w_here.at[k, :, cols], arrived.at[k, t])

    tiles = w_in.shape[1] // tile
    for t in range(tiles):
        for k in range(3):
            fetch(k, t).start()
    total = jnp.zeros((size, 1), f32)
    for k, src in enumerate((own, px, py)):
        for j in range(4):
            chunks[k, j * group : (j + 1) * group, :] = src[(j ^ k) * group : ((j ^ k) + 1) * group, :]
        wide = chunks[k].astype(f32)
        total = total + jnp.sum(wide * wide, axis=1, keepdims=True)
    square[...] = total

    @pl.loop(0, tiles)
    def _(t):
        cols = pl.ds(pl.multiple_of(t * tile, tile), tile)
        for k in range(3):
            fetch(k, t).wait()
        z[:, cols] = sum(jnp.dot(chunks[k], w_here[k, :, cols], preferred_element_type=f32) for k in range(3))


def far_kernel(size, tile, mp_ref, z, square, own, px, py, da, db, w_in, hidden, mine, chunk, scale):
    feat = own.shape[1]
    group = size // 4
    width = 4 * feat
    m = mp_ref[0]
    for j in range(4):
        src = db if j < 2 else da
        chunk[j * group : (j + 1) * group, :] = src[((j ^ 3) % 2) * group : ((j ^ 3) % 2 + 1) * group, :]
    wide = chunk[...].astype(f32)
    total = square[...] + jnp.sum(wide * wide, axis=1, keepdims=True)
    scale[...] = lax.rsqrt(total / width + norm_eps)
    rows = [pl.ds(pl.multiple_of((m ^ k) * feat, feat), feat) for k in range(4)]
    mine[:, rows[0]] = own[:group, :]
    mine[:, rows[1]] = px[group : 2 * group, :]
    mine[:, rows[2]] = py[2 * group : 3 * group, :]
    mine[:, rows[3]] = chunk[:group, :]

    @pl.loop(0, w_in.shape[1] // tile)
    def _(t):
        cols = pl.ds(pl.multiple_of(t * tile, tile), tile)
        total = z[:, cols] + jnp.dot(chunk[...], w_in[rows[3], cols], preferred_element_type=f32)
        hidden[:, cols] = jax.nn.gelu(total * scale[...]).astype(bf16)


def part_kernel(size, tile, hidden, w_out, send_a, send_b, keep_a, keep_b):
    group = size // 4
    half = w_out.shape[1] // 2
    for side in range(2):
        keep, send, order = ((keep_a, send_a, (0, 2, 1, 3)), (keep_b, send_b, (0, 1, 2, 3)))[side]

        @pl.loop(0, half // tile)
        def _(t):
            cols = pl.ds(pl.multiple_of(t * tile, tile), tile)
            from_cols = pl.ds(pl.multiple_of(t * tile + side * half, tile), tile)
            part = jnp.dot(hidden[...], w_out[:, from_cols], preferred_element_type=f32).astype(bf16)
            for i, j in enumerate(order):
                ref = keep if i < 2 else send
                ref[(i % 2) * group : (i % 2 + 1) * group, cols] = part[j * group : (j + 1) * group]


def fold_kernel(keep_a, got_a, keep_b, got_b, out_a, out_b):
    out_a[...] = (keep_a[...].astype(f32) + got_a[...].astype(f32)).astype(bf16)
    out_b[...] = (keep_b[...].astype(f32) + got_b[...].astype(f32)).astype(bf16)


def score_kernel(sections, cap, step_idx, mp_ref, mine, keep_a, got_a, last_a, keep_b, got_b, last_b, h0, h1_top, h1_bottom, h2_top, h2_bottom, h3_top, h3_bottom, notes, place, *rest):
    earlier, out = rest[:-1], rest[-1]
    group, width = mine.shape
    half = width // 2
    m = mp_ref[0]
    wide = lambda ref: ref[...].astype(f32)
    sum_a = keep_a[:group].astype(f32) + got_a[:group].astype(f32) + wide(last_a)
    sum_b = keep_b[:group].astype(f32) + got_b[:group].astype(f32) + wide(last_b)
    x = wide(mine)
    ha = x[:, :half] + sum_a
    hb = x[:, half:] + sum_b
    square = jnp.sum(ha * ha, axis=1, keepdims=True) + jnp.sum(hb * hb, axis=1, keepdims=True)
    scale = lax.rsqrt(square / width + norm_eps)
    na = (ha * scale).astype(bf16)
    nb = (hb * scale).astype(bf16)
    c = 4 * step_idx
    chosen = (notes[:, c : c + 1] * DIGIT + notes[:, c + 1 : c + 2]).astype(jnp.int32)
    logits = []
    heads = ((h0[:half], h0[half:]), (h1_top[...], h1_bottom[...]), (h2_top[...], h2_bottom[...]), (h3_top[...], h3_bottom[...]))
    for top, bottom in heads:
        logits.append(
            jnp.dot(na, top, preferred_element_type=f32) + jnp.dot(nb, bottom, preferred_element_type=f32)
        )
    peak = functools.reduce(jnp.maximum, [jnp.max(v, axis=1, keepdims=True) for v in logits])
    total = jnp.zeros((group, 1), f32)
    picked = jnp.zeros((group, 1), f32)
    for k, v in enumerate(logits):
        columns = iota(v.shape, 1) + (m ^ k) * v.shape[1]
        total = total + jnp.sum(jnp.exp(v - peak), axis=1, keepdims=True)
        picked = picked + jnp.sum(jnp.where(columns == chosen, v, 0.0), axis=1, keepdims=True)
    logp = picked - peak - jnp.log(total)
    slots = sections * cap
    spread = jnp.where(iota((group, slots), 0) == place[...], logp, 0.0)
    spread = jnp.sum(spread, axis=0, keepdims=True)
    if not earlier:
        for s in range(sections):
            out[s : s + 1, :] = spread[:, s * cap : (s + 1) * cap]
        return
    for s in range(sections):
        row = jnp.concatenate([earlier[0][s : s + 1, :], spread[:, s * cap : (s + 1) * cap]], axis=1)
        out[4 * s : 4 * s + 4, :] = jnp.broadcast_to(row, (4, 2 * cap))


def return_kernel(sections, cap, own_row, own_col, got, out):
    rows = own_row.shape[1]
    dest = own_row[...] * cap + slots_row(own_row[...], own_col[...])
    pick = (iota((sections * cap, rows), 0) == dest).astype(f32)
    agents = [jnp.sum(got[4 * a : 4 * a + 4, :], axis=0, keepdims=True) for a in range(sections)]
    steps = [jnp.concatenate([v[:, t * cap : (t + 1) * cap] for v in agents], axis=1) for t in range(STEPS)]
    steps = jnp.concatenate(steps + [jnp.zeros((8 - STEPS, sections * cap), f32)], axis=0)
    found = jnp.dot(steps, pick, precision=lax.Precision.HIGHEST, preferred_element_type=f32)
    out[...] = found[:STEPS]


def halves_kernel(source, top, bottom, done):
    h = top.shape[0]
    copies = [
        pltpu.make_async_copy(source.at[pl.ds(i * h, h)], half, done.at[i]) for i, half in enumerate((top, bottom))
    ]
    for copy in copies:
        copy.start()
    for copy in copies:
        copy.wait()


def call(kernel, outs, cost=None, **kw):
    return pl.pallas_call(
        kernel,
        out_shape=outs,
        compiler_params=pltpu.CompilerParams(vmem_limit_bytes=VMEM),
        cost_estimate=cost,
        **kw,
    )


def shape(*dims, dtype=bf16):
    return jax.ShapeDtypeStruct(dims, dtype)


SMEM_SPEC = pl.BlockSpec(memory_space=pltpu.SMEM)
VMEM_SPEC = pl.BlockSpec(memory_space=pltpu.VMEM)


def serve_rows(sections, cap, size, over_x, over_y, m, x0, x1, notes, place, w_in, w_out, *heads):
    feat = x0.shape[1]
    width = w_in.shape[0]
    inner = w_in.shape[1]
    group = size // 4

    h = size // 2
    flops = 2 * size * width * inner

    def near(v):
        return over_x(v), over_y(v)

    def far(from_x, from_y):
        return over_y(from_x[:h]), over_x(from_y[h:])

    def to_hidden(x, near_x, far_x):
        return call(
            functools.partial(hidden_kernel, size, TILE),
            (shape(size, inner), shape(group, width)),
            cost=pl.CostEstimate(flops=flops, bytes_accessed=2 * width * inner, transcendentals=size * inner),
            in_specs=[SMEM_SPEC] + [VMEM_SPEC] * 6,
            scratch_shapes=[pltpu.VMEM((size, width), bf16), pltpu.VMEM((size, 1), f32)],
        )(m, x, *near_x, *far_x, w_in)

    def to_near(x, near_x):
        return call(
            functools.partial(near_kernel, size, TILE),
            (shape(size, inner, dtype=f32), shape(size, 1, dtype=f32)),
            cost=pl.CostEstimate(flops=3 * flops // 4, bytes_accessed=2 * width * inner, transcendentals=0),
            in_specs=[SMEM_SPEC] + [VMEM_SPEC] * 3 + [pl.BlockSpec(memory_space=pl.ANY)],
            scratch_shapes=[
                pltpu.VMEM((3, size, feat), bf16),
                pltpu.VMEM((3, feat, inner), bf16),
                pltpu.SemaphoreType.DMA((3, inner // TILE)),
            ],
        )(m, x, *near_x, w_in)

    def finish_hidden(z, square, x, near_x, far_x):
        return call(
            functools.partial(far_kernel, size, TILE),
            (shape(size, inner), shape(group, width)),
            cost=pl.CostEstimate(flops=flops // 4, bytes_accessed=width * inner // 2, transcendentals=size * inner),
            in_specs=[SMEM_SPEC] + [VMEM_SPEC] * 8,
            scratch_shapes=[pltpu.VMEM((size, feat), bf16), pltpu.VMEM((size, 1), f32)],
        )(m, z, square, x, *near_x, *far_x, w_in)

    def to_parts(hidden):
        return call(
            functools.partial(part_kernel, size, TILE),
            (shape(h, width // 2),) * 4,
            cost=pl.CostEstimate(flops=flops, bytes_accessed=2 * width * inner, transcendentals=0),
        )(hidden, w_out)

    def fold(keep_a, got_a, keep_b, got_b):
        second = pl.BlockSpec((group, width // 2), lambda i: (1, 0))
        whole = pl.BlockSpec((group, width // 2), lambda i: (0, 0))
        return call(
            fold_kernel,
            (shape(group, width // 2),) * 2,
            grid=(1,),
            in_specs=[second] * 4,
            out_specs=(whole,) * 2,
        )(keep_a, got_a, keep_b, got_b)

    def score(step_idx, pieces, *earlier):
        return call(
            functools.partial(score_kernel, sections, cap, step_idx),
            shape(4 * sections, 2 * cap, dtype=f32) if earlier else shape(sections, cap, dtype=f32),
            in_specs=[SMEM_SPEC] + [VMEM_SPEC] * (9 + len(heads) + len(earlier)),
        )(m, *pieces, *heads, notes, place, *earlier)

    x0, x1, notes = x0[:size], x1[:size], notes[:group]
    near0 = near(x0)
    far0 = far(*near0)
    z0, square0 = to_near(x0, near0)
    x1, *near0 = lax.optimization_barrier((x1, *near0))
    near1 = near(x1)
    z0, *near1 = lax.optimization_barrier((z0, *near1))
    hidden0, mine0 = finish_hidden(z0, square0, x0, near0, far0)
    far1 = far(*near1)
    send_a0, send_b0, keep_a0, keep_b0 = to_parts(hidden0)
    got_a0, got_b0 = over_x(send_a0), over_y(send_b0)
    hidden1, mine1 = to_hidden(x1, near1, far1)
    hidden1, got_a0, got_b0 = lax.optimization_barrier((hidden1, got_a0, got_b0))
    fold_a0, fold_b0 = fold(keep_a0, got_a0, keep_b0, got_b0)
    last_a0, last_b0 = over_y(fold_a0), over_x(fold_b0)
    hidden1, fold_a0 = lax.optimization_barrier((hidden1, fold_a0))
    send_a1, send_b1, keep_a1, keep_b1 = to_parts(hidden1)
    got_a1, got_b1 = over_x(send_a1), over_y(send_b1)
    fold_a1, fold_b1 = fold(keep_a1, got_a1, keep_b1, got_b1)
    last_a1, last_b1 = over_y(fold_a1), over_x(fold_b1)
    first = score(0, (mine0, keep_a0, got_a0, last_a0, keep_b0, got_b0, last_b0))
    return score(1, (mine1, keep_a1, got_a1, last_a1, keep_b1, got_b1, last_b1), first)


def plane_plan(matches, actions, state, embed, w_in, w_out, head):
    sections = lax.axis_size("section")
    games, _, feat = state.shape
    cap = 4 * games // sections
    rows = 2 * games
    slots = sections * cap
    width = 4 * feat
    m = lax.axis_index("mp").astype(jnp.int32).reshape(1)
    over_x = lambda v: lax.ppermute(v, "mp", [(i, i ^ 1) for i in range(4)])
    over_y = lambda v: lax.ppermute(v, "mp", [(i, i ^ 2) for i in range(4)])

    own_row = matches.T.reshape(1, rows)
    own_col = own_row.reshape(rows, 1)
    acts = actions.transpose(0, 2, 1)
    mine0, other0, mine1 = acts[0].reshape(rows), acts[0, ::-1].reshape(rows), acts[1].reshape(rows)
    notes = jnp.stack(
        [
            mine0 // DIGIT, mine0 % DIGIT, other0 // DIGIT, other0 % DIGIT,
            mine1 // DIGIT, mine1 % DIGIT, jnp.zeros_like(mine0), jnp.ones_like(mine0),
        ]
    ).astype(bf16)

    head_own = head[0]
    rows_half = head_own.shape[0] // 2
    top, bottom = call(
        halves_kernel,
        (shape(rows_half, head_own.shape[1]),) * 2,
        in_specs=[pl.BlockSpec(memory_space=pl.ANY)],
        scratch_shapes=[pltpu.SemaphoreType.DMA((2,))],
    )(head_own)
    x_top, y_bottom = over_x(top), over_y(bottom)
    others = (x_top, over_x(bottom), over_y(top), y_bottom, over_y(x_top), over_x(y_bottom))

    packed = call(functools.partial(pack_kernel, sections, cap), shape(sections, cap + META, feat))(
        own_row, own_col, notes, state
    )
    arrived = lax.all_to_all(packed, "section", split_axis=0, concat_axis=0, tiled=True)
    x0, x1, notes_c, place, count = call(
        functools.partial(unpack_kernel, sections, cap),
        (
            shape(slots, feat), shape(slots, feat), shape(slots // 4, META, dtype=f32),
            shape(1, slots, dtype=jnp.int32), shape(1, dtype=jnp.int32),
        ),
        in_specs=[SMEM_SPEC, VMEM_SPEC, VMEM_SPEC],
        out_specs=(VMEM_SPEC,) * 4 + (SMEM_SPEC,),
    )(m, arrived, embed)

    x0, *others = lax.optimization_barrier((x0,) + others)
    heads = (head_own, *others)

    branches = [
        functools.partial(serve_rows, sections, cap, slots * num // den, over_x, over_y) for num, den in SHARES
    ]
    sent = lax.switch(count[0], branches, m, x0, x1, notes_c, place, w_in[0, 0], w_out[0, 0], *heads)
    back = lax.all_to_all(sent, ("section", "mp"), split_axis=0, concat_axis=0, tiled=True)
    logp = call(functools.partial(return_kernel, sections, cap), shape(STEPS, rows, dtype=f32))(own_row, own_col, back)
    return logp.reshape(STEPS, 2, games).transpose(0, 2, 1)


def general_plan(matches, actions, state, embed, w_in, w_out, head):
    sections = lax.axis_size("section")
    game_count = matches.shape[0]
    feat_width = state.shape[2]
    slot_cap = 4 * game_count // sections
    served = sections * slot_cap
    owners = matches.reshape(-1)
    onehot = (owners[:, None] == jnp.arange(sections, dtype=jnp.int32)[None, :]).astype(jnp.int32)
    slot_of = jnp.sum((jnp.cumsum(onehot, axis=0) - onehot) * onehot, axis=1)
    action_width = head.shape[2]
    columns = lax.axis_index("mp") * action_width + jnp.arange(action_width, dtype=jnp.int32)
    current = state
    results = []
    for step_idx in range(STEPS):
        observed = current.astype(bf16).reshape(2 * game_count, feat_width)
        outgoing = jnp.zeros((sections, slot_cap, feat_width), bf16).at[owners, slot_of].set(observed)
        arrived = lax.all_to_all(outgoing, "section", split_axis=0, concat_axis=0, tiled=True)
        inputs = lax.all_gather(arrived.reshape(served, feat_width), "mp", axis=1, tiled=True)
        normed = rms_round(inputs)
        hidden = jax.nn.gelu(jnp.dot(normed, w_in[0, 0], preferred_element_type=f32)).astype(bf16)
        partial_value = jnp.dot(hidden, w_out[0, 0], preferred_element_type=f32)
        summed = inputs.astype(f32) + lax.psum(partial_value.astype(bf16), "mp").astype(f32)
        logits = jnp.dot(rms_round(summed), head[0], preferred_element_type=f32)
        returned = lax.all_to_all(
            logits.reshape(sections, slot_cap, action_width).astype(bf16),
            "section",
            split_axis=0,
            concat_axis=0,
            tiled=True,
        ).astype(f32)
        row_logits = returned[owners, slot_of]
        row_peak = lax.pmax(jnp.max(row_logits, axis=1), "mp")
        chosen = actions[step_idx].reshape(-1)
        local_total = jnp.sum(jnp.exp(row_logits - row_peak[:, None]), axis=1)
        local_pick = jnp.sum(jnp.where(columns[None, :] == chosen[:, None], row_logits, 0.0), axis=1)
        row_total, picked = lax.psum((local_total, local_pick), "mp")
        results.append((picked - row_peak - jnp.log(row_total)).reshape(game_count, 2))
        picked_rows = jnp.take(embed, actions[step_idx], axis=0).astype(f32)
        current = 0.8 * current + picked_rows + 0.5 * picked_rows[:, ::-1, :]
    return jnp.stack(results)


def solution(mesh):
    return jax.shard_map(
        plane_plan if mesh.shape["mp"] == 4 else general_plan,
        mesh=mesh,
        in_specs=(
            P("section", None),
            P(None, "section", None),
            P("section", None, "mp"),
            P(None, "mp"),
            P("section", None, None, "mp"),
            P("section", None, "mp", None),
            P("section", None, "mp"),
        ),
        out_specs=P(None, "section", None),
        check_vma=False,
    )
```

```python
import functools

import jax
import jax.numpy as jnp
from jax import lax
from jax.experimental import pallas as pl
from jax.experimental.pallas import tpu as pltpu
from jax.sharding import PartitionSpec as P

STEPS = 2
META = 8
DIGIT = 32
SHARES = ((1, 1), (3, 4), (1, 2))
TILE = 512
VMEM = 20 * 1024 * 1024

norm_eps = 1e-06
f32 = jnp.float32
bf16 = jnp.bfloat16


def rms_round(source):
    widened = source.astype(f32)
    scale = lax.rsqrt(jnp.mean(widened * widened, axis=-1, keepdims=True) + norm_eps)
    return (widened * scale).astype(bf16)


def iota(shape, dim):
    return lax.broadcasted_iota(jnp.int32, shape, dim)


def nt_dot(left, right):
    return lax.dot_general(left, right, (((1,), (1,)), ((), ())), preferred_element_type=f32)


def slots_row(own_row):
    rows = own_row.shape[1]
    lower, upper = iota((rows, rows), 0), iota((rows, rows), 1)
    own_col = jnp.sum(jnp.where(lower == upper, own_row, 0), axis=1, keepdims=True)
    earlier = (own_col == own_row) & (lower < upper)
    return jnp.sum(earlier.astype(jnp.int32), axis=0, keepdims=True)


def owners_row(pair):
    return jnp.concatenate([pair[0:1, :], pair[1:2, :]], axis=1)


def pack_kernel(sections, cap, agents, acts, state, out, agents_here, acts_here, state_here, done):
    copies = [
        pltpu.make_async_copy(far, here, done.at[i])
        for i, (far, here) in enumerate(((agents, agents_here), (acts, acts_here), (state, state_here)))
    ]
    for copy in copies:
        copy.start()
    games, _, feat = state_here.shape
    rows = 2 * games
    copies[0].wait()
    own_row = owners_row(agents_here)
    dest = own_row * cap + slots_row(own_row)
    select = (iota((sections * cap, rows), 0) == dest).astype(bf16)
    copies[1].wait()
    first, second = (acts_here[0, p : p + 1, :] for p in range(2))
    mine0 = jnp.concatenate([first, second], axis=1)
    other0 = jnp.concatenate([second, first], axis=1)
    mine1 = jnp.concatenate([acts_here[1, 0:1, :], acts_here[1, 1:2, :]], axis=1)
    digits = [v for a in (mine0, other0, mine1) for v in (a // DIGIT, a % DIGIT)]
    meta = jnp.concatenate(digits + [jnp.zeros_like(mine0), jnp.ones_like(mine0)], axis=0).astype(f32).astype(bf16)
    notes = nt_dot(meta, select).astype(bf16)
    copies[2].wait()
    packed = jnp.dot(select[:, :games], state_here[:, 0, :].astype(bf16), preferred_element_type=f32)
    packed = packed + jnp.dot(select[:, games:], state_here[:, 1, :].astype(bf16), preferred_element_type=f32)
    packed = packed.astype(bf16)
    for s in range(sections):
        out[s, :cap, :] = packed[s * cap : (s + 1) * cap]
        out[s, cap:, :] = jnp.zeros((META, feat), bf16)
        out[s, cap:, :cap] = notes[:, s * cap : (s + 1) * cap]


def unpack_kernel(sections, cap, mp_ref, arrived, embed, x0_out, x1_out, notes_out, place_out, count_out):
    slots = sections * cap
    m = mp_ref[0]
    rows = jnp.concatenate([arrived[s, :cap, :] for s in range(sections)], axis=0)
    notes = jnp.concatenate([arrived[s, cap:, :cap] for s in range(sections)], axis=1)
    live = notes[META - 1 : META, :].astype(f32)
    before = (iota((slots, slots), 0) < iota((slots, slots), 1)).astype(bf16)
    rank = jnp.dot(jnp.broadcast_to(live, (8, slots)).astype(bf16), before, preferred_element_type=f32)
    rank = rank[:1].astype(jnp.int32)
    served = jnp.sum(live).astype(jnp.int32)
    fits = [(served * den <= slots * num).astype(jnp.int32) for num, den in SHARES]
    count_out[0] = sum(fits[1:], 0)
    group = slots // 4
    for (num, den), fit in zip(SHARES[1:], fits[1:]):
        group = group + fit * (slots * num // den // 4 - group)
    block = sum((rank >= j * group).astype(jnp.int32) for j in range(1, 4))
    place = jnp.where(live > 0, (block ^ m) * group + (rank - block * group), -1)
    size = slots
    select = (iota((size, slots), 0) == place).astype(bf16)
    x0 = jnp.dot(select, rows, preferred_element_type=f32)
    mine = nt_dot(select, notes)
    own = (mine[:, 0:1] * DIGIT + mine[:, 1:2]).astype(jnp.int32)
    other = (mine[:, 2:3] * DIGIT + mine[:, 3:4]).astype(jnp.int32)
    columns = iota((size, embed.shape[0]), 1)
    effect = jnp.where(columns == own, 1.0, 0.0) + jnp.where(columns == other, 0.5, 0.0)
    moved = jnp.dot(effect.astype(bf16), embed[...], preferred_element_type=f32)
    x0_out[...] = x0.astype(bf16)
    x1_out[...] = (0.8 * x0 + moved).astype(bf16)
    notes_out[...] = mine[: size // 4]
    place_out[...] = place


def hidden_kernel(size, tile, mp_ref, own, px, py, da, db, w_in, hidden, mine, x_full, scale):
    feat = own.shape[1]
    group = size // 4
    width, inner = w_in.shape
    m = mp_ref[0]
    total = jnp.zeros((size, 1), f32)
    for k in range(4):
        parts = []
        for j in range(4):
            b = j ^ k
            if k == 3:
                src = da if b < 2 else db
                parts.append(src[(b % 2) * group : (b % 2 + 1) * group, :])
            else:
                src = (own, px, py)[k]
                parts.append(src[b * group : (b + 1) * group, :])
        chunk = jnp.concatenate(parts, axis=0)
        x_full[:, pl.ds(pl.multiple_of((m ^ k) * feat, feat), feat)] = chunk
        wide = chunk.astype(f32)
        total = total + jnp.sum(wide * wide, axis=1, keepdims=True)
    scale[...] = lax.rsqrt(total / width + norm_eps)
    mine[...] = x_full[:group, :]

    @pl.loop(0, inner // tile)
    def _(t):
        cols = pl.ds(pl.multiple_of(t * tile, tile), tile)
        z = jnp.dot(x_full[...], w_in[:, cols], preferred_element_type=f32)
        hidden[:, cols] = jax.nn.gelu(z * scale[...]).astype(bf16)


def near_kernel(size, tile, mp_ref, own, px, py, w_in, *rest):
    *ends, chunks, w_here, arrived, halved = rest
    halves = []
    if len(ends) == 6:
        first, second, z, square, left, right = ends
        h = left.shape[0]
        halves.append(pltpu.make_async_copy(first.at[pl.ds(0, h)], left, halved.at[0]))
        halves.append(pltpu.make_async_copy(second.at[pl.ds(h, h)], right, halved.at[1]))
    else:
        z, square = ends
    feat = own.shape[1]
    group = size // 4
    m = mp_ref[0]

    def fetch(k, t):
        rows = pl.ds(pl.multiple_of((m ^ k) * feat, feat), feat)
        cols = pl.ds(pl.multiple_of(t * tile, tile), tile)
        return pltpu.make_async_copy(w_in.at[rows, cols], w_here.at[k, :, cols], arrived.at[k, t])

    tiles = w_in.shape[1] // tile
    for t in range(tiles):
        for k in range(3):
            fetch(k, t).start()
    for copy in halves:
        copy.start()
    total = jnp.zeros((size, 1), f32)
    for k, src in enumerate((own, px, py)):
        for j in range(4):
            chunks[k, j * group : (j + 1) * group, :] = src[(j ^ k) * group : ((j ^ k) + 1) * group, :]
        wide = chunks[k].astype(f32)
        total = total + jnp.sum(wide * wide, axis=1, keepdims=True)
    square[...] = total

    @pl.loop(0, tiles)
    def _(t):
        cols = pl.ds(pl.multiple_of(t * tile, tile), tile)
        for k in range(3):
            fetch(k, t).wait()
        z[:, cols] = sum(jnp.dot(chunks[k], w_here[k, :, cols], preferred_element_type=f32) for k in range(3))

    for copy in halves:
        copy.wait()


def far_kernel(size, tile, mp_ref, z, square, own, px, py, da, db, w_in, hidden, mine, chunk, scale):
    feat = own.shape[1]
    group = size // 4
    width = 4 * feat
    m = mp_ref[0]
    for j in range(4):
        src = db if j < 2 else da
        chunk[j * group : (j + 1) * group, :] = src[((j ^ 3) % 2) * group : ((j ^ 3) % 2 + 1) * group, :]
    wide = chunk[...].astype(f32)
    total = square[...] + jnp.sum(wide * wide, axis=1, keepdims=True)
    scale[...] = lax.rsqrt(total / width + norm_eps)
    rows = [pl.ds(pl.multiple_of((m ^ k) * feat, feat), feat) for k in range(4)]
    mine[:, rows[0]] = own[:group, :]
    mine[:, rows[1]] = px[group : 2 * group, :]
    mine[:, rows[2]] = py[2 * group : 3 * group, :]
    mine[:, rows[3]] = chunk[:group, :]

    @pl.loop(0, w_in.shape[1] // tile)
    def _(t):
        cols = pl.ds(pl.multiple_of(t * tile, tile), tile)
        total = z[:, cols] + jnp.dot(chunk[...], w_in[rows[3], cols], preferred_element_type=f32)
        hidden[:, cols] = jax.nn.gelu(total * scale[...]).astype(bf16)


def part_kernel(size, tile, hidden, w_out, send_a, send_b, keep_a, keep_b):
    group = size // 4
    half = w_out.shape[1] // 2
    for side in range(2):
        keep, send, order = ((keep_a, send_a, (0, 2, 1, 3)), (keep_b, send_b, (0, 1, 2, 3)))[side]

        @pl.loop(0, half // tile)
        def _(t):
            cols = pl.ds(pl.multiple_of(t * tile, tile), tile)
            from_cols = pl.ds(pl.multiple_of(t * tile + side * half, tile), tile)
            part = jnp.dot(hidden[...], w_out[:, from_cols], preferred_element_type=f32).astype(bf16)
            for i, j in enumerate(order):
                ref = keep if i < 2 else send
                ref[(i % 2) * group : (i % 2 + 1) * group, cols] = part[j * group : (j + 1) * group]


def fold_kernel(keep_a, got_a, keep_b, got_b, out_a, out_b):
    out_a[...] = (keep_a[...].astype(f32) + got_a[...].astype(f32)).astype(bf16)
    out_b[...] = (keep_b[...].astype(f32) + got_b[...].astype(f32)).astype(bf16)


def score_kernel(sections, cap, step_idx, mp_ref, mine, keep_a, got_a, last_a, keep_b, got_b, last_b, h0, h1, h2, h3_top, h3_bottom, notes, place, *rest):
    earlier, out = rest[:-1], rest[-1]
    group, width = mine.shape
    half = width // 2
    m = mp_ref[0]
    wide = lambda ref: ref[...].astype(f32)
    sum_a = keep_a[:group].astype(f32) + got_a[:group].astype(f32) + wide(last_a)
    sum_b = keep_b[:group].astype(f32) + got_b[:group].astype(f32) + wide(last_b)
    x = wide(mine)
    ha = x[:, :half] + sum_a
    hb = x[:, half:] + sum_b
    square = jnp.sum(ha * ha, axis=1, keepdims=True) + jnp.sum(hb * hb, axis=1, keepdims=True)
    scale = lax.rsqrt(square / width + norm_eps)
    na = (ha * scale).astype(bf16)
    nb = (hb * scale).astype(bf16)
    c = 4 * step_idx
    chosen = (notes[:, c : c + 1] * DIGIT + notes[:, c + 1 : c + 2]).astype(jnp.int32)
    logits = []
    heads = ((h0[:half], h0[half:]), (h1[:half], h1[half:]), (h2[:half], h2[half:]), (h3_top[...], h3_bottom[...]))
    for top, bottom in heads:
        logits.append(
            jnp.dot(na, top, preferred_element_type=f32) + jnp.dot(nb, bottom, preferred_element_type=f32)
        )
    peak = functools.reduce(jnp.maximum, [jnp.max(v, axis=1, keepdims=True) for v in logits])
    total = jnp.zeros((group, 1), f32)
    picked = jnp.zeros((group, 1), f32)
    for k, v in enumerate(logits):
        columns = iota(v.shape, 1) + (m ^ k) * v.shape[1]
        total = total + jnp.sum(jnp.exp(v - peak), axis=1, keepdims=True)
        picked = picked + jnp.sum(jnp.where(columns == chosen, v, 0.0), axis=1, keepdims=True)
    logp = picked - peak - jnp.log(total)
    slots = sections * cap
    spread = jnp.where(iota((group, slots), 0) == place[...], logp, 0.0)
    spread = jnp.sum(spread, axis=0, keepdims=True)
    if not earlier:
        for s in range(sections):
            out[s : s + 1, :] = spread[:, s * cap : (s + 1) * cap]
        return
    for s in range(sections):
        row = jnp.concatenate([earlier[0][s : s + 1, :], spread[:, s * cap : (s + 1) * cap]], axis=1)
        out[4 * s : 4 * s + 4, :] = jnp.broadcast_to(row, (4, 2 * cap))


def return_kernel(sections, cap, agents, got, out):
    own_row = owners_row(agents)
    rows = own_row.shape[1]
    dest = own_row * cap + slots_row(own_row)
    pick = (iota((sections * cap, rows), 0) == dest).astype(f32)
    sums = [jnp.sum(got[4 * a : 4 * a + 4, :], axis=0, keepdims=True) for a in range(sections)]
    steps = [jnp.concatenate([v[:, t * cap : (t + 1) * cap] for v in sums], axis=1) for t in range(STEPS)]
    steps = jnp.concatenate(steps + [jnp.zeros((8 - STEPS, sections * cap), f32)], axis=0)
    found = jnp.dot(steps, pick, precision=lax.Precision.HIGHEST, preferred_element_type=f32)
    out[...] = found[:STEPS]


def call(kernel, outs, cost=None, **kw):
    return pl.pallas_call(
        kernel,
        out_shape=outs,
        compiler_params=pltpu.CompilerParams(vmem_limit_bytes=VMEM),
        cost_estimate=cost,
        **kw,
    )


def shape(*dims, dtype=bf16):
    return jax.ShapeDtypeStruct(dims, dtype)


SMEM_SPEC = pl.BlockSpec(memory_space=pltpu.SMEM)
HBM_SPEC = pl.BlockSpec(memory_space=pltpu.HBM)
VMEM_SPEC = pl.BlockSpec(memory_space=pltpu.VMEM)


def serve_rows(sections, cap, size, over_x, over_y, m, x0, x1, notes, place, w_in, w_out, *heads):
    feat = x0.shape[1]
    width = w_in.shape[0]
    inner = w_in.shape[1]
    group = size // 4

    h = size // 2
    flops = 2 * size * width * inner

    def near(v):
        return over_x(v), over_y(v)

    def far(from_x, from_y):
        return over_y(from_x[:h]), over_x(from_y[h:])

    def to_hidden(x, near_x, far_x):
        return call(
            functools.partial(hidden_kernel, size, TILE),
            (shape(size, inner), shape(group, width)),
            cost=pl.CostEstimate(flops=flops, bytes_accessed=2 * width * inner, transcendentals=size * inner),
            in_specs=[SMEM_SPEC] + [VMEM_SPEC] * 6,
            scratch_shapes=[pltpu.VMEM((size, width), bf16), pltpu.VMEM((size, 1), f32)],
        )(m, x, *near_x, *far_x, w_in)

    def to_near(x, near_x, *wholes):
        halves = tuple(shape(v.shape[0] // 2, v.shape[1]) for v in wholes)
        any_spec = pl.BlockSpec(memory_space=pl.ANY)
        return call(
            functools.partial(near_kernel, size, TILE),
            (shape(size, inner, dtype=f32), shape(size, 1, dtype=f32)) + halves,
            cost=pl.CostEstimate(flops=3 * flops // 4, bytes_accessed=2 * width * inner, transcendentals=0),
            in_specs=[SMEM_SPEC] + [VMEM_SPEC] * 3 + [any_spec] * (1 + len(wholes)),
            out_specs=(VMEM_SPEC,) * 2 + (any_spec,) * len(halves),
            scratch_shapes=[
                pltpu.VMEM((3, size, feat), bf16),
                pltpu.VMEM((3, feat, inner), bf16),
                pltpu.SemaphoreType.DMA((3, inner // TILE)),
                pltpu.SemaphoreType.DMA((2,)),
            ],
        )(m, x, *near_x, w_in, *wholes)

    def finish_hidden(z, square, x, near_x, far_x):
        return call(
            functools.partial(far_kernel, size, TILE),
            (shape(size, inner), shape(group, width)),
            cost=pl.CostEstimate(flops=flops // 4, bytes_accessed=width * inner // 2, transcendentals=size * inner),
            in_specs=[SMEM_SPEC] + [VMEM_SPEC] * 8,
            scratch_shapes=[pltpu.VMEM((size, feat), bf16), pltpu.VMEM((size, 1), f32)],
        )(m, z, square, x, *near_x, *far_x, w_in)

    def to_parts(hidden):
        return call(
            functools.partial(part_kernel, size, TILE),
            (shape(h, width // 2),) * 4,
            cost=pl.CostEstimate(flops=flops, bytes_accessed=2 * width * inner, transcendentals=0),
        )(hidden, w_out)

    def fold(keep_a, got_a, keep_b, got_b):
        second = pl.BlockSpec((group, width // 2), lambda i: (1, 0))
        whole = pl.BlockSpec((group, width // 2), lambda i: (0, 0))
        return call(
            fold_kernel,
            (shape(group, width // 2),) * 2,
            grid=(1,),
            in_specs=[second] * 4,
            out_specs=(whole,) * 2,
        )(keep_a, got_a, keep_b, got_b)

    def score(step_idx, pieces, *earlier):
        return call(
            functools.partial(score_kernel, sections, cap, step_idx),
            shape(4 * sections, 2 * cap, dtype=f32) if earlier else shape(sections, cap, dtype=f32),
            in_specs=[SMEM_SPEC] + [VMEM_SPEC] * (14 + len(earlier)),
        )(m, *pieces, head_own, head_x, head_y, *head_far, notes, place, *earlier)

    x0, x1, notes = x0[:size], x1[:size], notes[:group]
    near0 = near(x0)
    far0 = far(*near0)
    head_own, head_x, head_y = heads
    z0, square0, left, right = to_near(x0, near0, head_x, head_y)
    x1, *near0 = lax.optimization_barrier((x1, *near0))
    near1 = near(x1)
    z0, left, right, *near1 = lax.optimization_barrier((z0, left, right, *near1))
    head_far = over_y(left), over_x(right)
    hidden0, mine0 = finish_hidden(z0, square0, x0, near0, far0)
    far1 = far(*near1)
    send_a0, send_b0, keep_a0, keep_b0 = to_parts(hidden0)
    got_a0, got_b0 = over_x(send_a0), over_y(send_b0)
    hidden1, mine1 = to_hidden(x1, near1, far1)
    hidden1, got_a0, got_b0 = lax.optimization_barrier((hidden1, got_a0, got_b0))
    fold_a0, fold_b0 = fold(keep_a0, got_a0, keep_b0, got_b0)
    last_a0, last_b0 = over_y(fold_a0), over_x(fold_b0)
    hidden1, fold_a0 = lax.optimization_barrier((hidden1, fold_a0))
    send_a1, send_b1, keep_a1, keep_b1 = to_parts(hidden1)
    got_a1, got_b1 = over_x(send_a1), over_y(send_b1)
    got_a1, *head_far = lax.optimization_barrier((got_a1, *head_far))
    fold_a1, fold_b1 = fold(keep_a1, got_a1, keep_b1, got_b1)
    last_a1, last_b1 = over_y(fold_a1), over_x(fold_b1)
    first = score(0, (mine0, keep_a0, got_a0, last_a0, keep_b0, got_b0, last_b0))
    return score(1, (mine1, keep_a1, got_a1, last_a1, keep_b1, got_b1, last_b1), first)


def plane_plan(matches, actions, state, embed, w_in, w_out, head):
    sections = lax.axis_size("section")
    games, _, feat = state.shape
    cap = 4 * games // sections
    rows = 2 * games
    slots = sections * cap
    width = 4 * feat
    m = lax.axis_index("mp").astype(jnp.int32).reshape(1)
    over_x = lambda v: lax.ppermute(v, "mp", [(i, i ^ 1) for i in range(4)])
    over_y = lambda v: lax.ppermute(v, "mp", [(i, i ^ 2) for i in range(4)])

    agents = matches.T
    acts = actions.transpose(0, 2, 1)

    head_own = head[0]
    head_x, head_y = over_x(head_own), over_y(head_own)
    others = (head_x, head_y)

    packed = call(
        functools.partial(pack_kernel, sections, cap),
        shape(sections, cap + META, feat),
        in_specs=[HBM_SPEC] * 3,
        scratch_shapes=[
            pltpu.VMEM(agents.shape, jnp.int32),
            pltpu.VMEM(acts.shape, jnp.int32),
            pltpu.VMEM(state.shape, f32),
            pltpu.SemaphoreType.DMA((3,)),
        ],
    )(agents, acts, state)
    arrived = lax.all_to_all(packed, "section", split_axis=0, concat_axis=0, tiled=True)
    x0, x1, notes_c, place, count = call(
        functools.partial(unpack_kernel, sections, cap),
        (
            shape(slots, feat), shape(slots, feat), shape(slots // 4, META, dtype=f32),
            shape(1, slots, dtype=jnp.int32), shape(1, dtype=jnp.int32),
        ),
        in_specs=[SMEM_SPEC, VMEM_SPEC, VMEM_SPEC],
        out_specs=(VMEM_SPEC,) * 4 + (SMEM_SPEC,),
    )(m, arrived, embed)

    x0, *others = lax.optimization_barrier((x0,) + others)
    heads = (head_own, *others)

    branches = [
        functools.partial(serve_rows, sections, cap, slots * num // den, over_x, over_y) for num, den in SHARES
    ]
    sent = lax.switch(count[0], branches, m, x0, x1, notes_c, place, w_in[0, 0], w_out[0, 0], *heads)
    back = lax.all_to_all(sent, ("section", "mp"), split_axis=0, concat_axis=0, tiled=True)
    logp = call(functools.partial(return_kernel, sections, cap), shape(STEPS, rows, dtype=f32))(agents, back)
    return logp.reshape(STEPS, 2, games).transpose(0, 2, 1)


def general_plan(matches, actions, state, embed, w_in, w_out, head):
    sections = lax.axis_size("section")
    game_count = matches.shape[0]
    feat_width = state.shape[2]
    slot_cap = 4 * game_count // sections
    served = sections * slot_cap
    owners = matches.reshape(-1)
    onehot = (owners[:, None] == jnp.arange(sections, dtype=jnp.int32)[None, :]).astype(jnp.int32)
    slot_of = jnp.sum((jnp.cumsum(onehot, axis=0) - onehot) * onehot, axis=1)
    action_width = head.shape[2]
    columns = lax.axis_index("mp") * action_width + jnp.arange(action_width, dtype=jnp.int32)
    current = state
    results = []
    for step_idx in range(STEPS):
        observed = current.astype(bf16).reshape(2 * game_count, feat_width)
        outgoing = jnp.zeros((sections, slot_cap, feat_width), bf16).at[owners, slot_of].set(observed)
        arrived = lax.all_to_all(outgoing, "section", split_axis=0, concat_axis=0, tiled=True)
        inputs = lax.all_gather(arrived.reshape(served, feat_width), "mp", axis=1, tiled=True)
        normed = rms_round(inputs)
        hidden = jax.nn.gelu(jnp.dot(normed, w_in[0, 0], preferred_element_type=f32)).astype(bf16)
        partial_value = jnp.dot(hidden, w_out[0, 0], preferred_element_type=f32)
        summed = inputs.astype(f32) + lax.psum(partial_value.astype(bf16), "mp").astype(f32)
        logits = jnp.dot(rms_round(summed), head[0], preferred_element_type=f32)
        returned = lax.all_to_all(
            logits.reshape(sections, slot_cap, action_width).astype(bf16),
            "section",
            split_axis=0,
            concat_axis=0,
            tiled=True,
        ).astype(f32)
        row_logits = returned[owners, slot_of]
        row_peak = lax.pmax(jnp.max(row_logits, axis=1), "mp")
        chosen = actions[step_idx].reshape(-1)
        local_total = jnp.sum(jnp.exp(row_logits - row_peak[:, None]), axis=1)
        local_pick = jnp.sum(jnp.where(columns[None, :] == chosen[:, None], row_logits, 0.0), axis=1)
        row_total, picked = lax.psum((local_total, local_pick), "mp")
        results.append((picked - row_peak - jnp.log(row_total)).reshape(game_count, 2))
        picked_rows = jnp.take(embed, actions[step_idx], axis=0).astype(f32)
        current = 0.8 * current + picked_rows + 0.5 * picked_rows[:, ::-1, :]
    return jnp.stack(results)


def solution(mesh):
    return jax.shard_map(
        plane_plan if mesh.shape["mp"] == 4 else general_plan,
        mesh=mesh,
        in_specs=(
            P("section", None),
            P(None, "section", None),
            P("section", None, "mp"),
            P(None, "mp"),
            P("section", None, None, "mp"),
            P("section", None, "mp", None),
            P("section", None, "mp"),
        ),
        out_specs=P(None, "section", None),
        check_vma=False,
    )
```

```python
import functools

import jax
import jax.numpy as jnp
from jax import lax
from jax.experimental import pallas as pl
from jax.experimental.pallas import tpu as pltpu
from jax.sharding import PartitionSpec as P

STEPS = 2
META = 8
DIGIT = 32
SHARES = ((1, 1), (5, 8), (3, 8))
TILE = 512
VMEM = 20 * 1024 * 1024

norm_eps = 1e-06
f32 = jnp.float32
bf16 = jnp.bfloat16


def rms_round(source):
    widened = source.astype(f32)
    scale = lax.rsqrt(jnp.mean(widened * widened, axis=-1, keepdims=True) + norm_eps)
    return (widened * scale).astype(bf16)


def iota(shape, dim):
    return lax.broadcasted_iota(jnp.int32, shape, dim)


def nt_dot(left, right):
    return lax.dot_general(left, right, (((1,), (1,)), ((), ())), preferred_element_type=f32)


def slots_row(own_row):
    rows = own_row.shape[1]
    lower, upper = iota((rows, rows), 0), iota((rows, rows), 1)
    own_col = jnp.sum(jnp.where(lower == upper, own_row, 0), axis=1, keepdims=True)
    earlier = (own_col == own_row) & (lower < upper)
    return jnp.sum(earlier.astype(jnp.int32), axis=0, keepdims=True)


def owners_row(pair):
    return jnp.concatenate([pair[0:1, :], pair[1:2, :]], axis=1)


def pack_kernel(sections, cap, agents, acts, state, out, agents_here, acts_here, state_here, done):
    copies = [
        pltpu.make_async_copy(far, here, done.at[i])
        for i, (far, here) in enumerate(((agents, agents_here), (acts, acts_here), (state, state_here)))
    ]
    for copy in copies:
        copy.start()
    games, _, feat = state_here.shape
    rows = 2 * games
    copies[0].wait()
    own_row = owners_row(agents_here)
    dest = own_row * cap + slots_row(own_row)
    select = (iota((sections * cap, rows), 0) == dest).astype(bf16)
    copies[1].wait()
    first, second = (acts_here[0, p : p + 1, :] for p in range(2))
    mine0 = jnp.concatenate([first, second], axis=1)
    other0 = jnp.concatenate([second, first], axis=1)
    mine1 = jnp.concatenate([acts_here[1, 0:1, :], acts_here[1, 1:2, :]], axis=1)
    digits = [v for a in (mine0, other0, mine1) for v in (a // DIGIT, a % DIGIT)]
    meta = jnp.concatenate(digits + [jnp.zeros_like(mine0), jnp.ones_like(mine0)], axis=0).astype(f32).astype(bf16)
    notes = nt_dot(meta, select).astype(bf16)
    copies[2].wait()
    packed = jnp.dot(select[:, :games], state_here[:, 0, :].astype(bf16), preferred_element_type=f32)
    packed = packed + jnp.dot(select[:, games:], state_here[:, 1, :].astype(bf16), preferred_element_type=f32)
    packed = packed.astype(bf16)
    for s in range(sections):
        out[s, :cap, :] = packed[s * cap : (s + 1) * cap]
        out[s, cap:, :] = jnp.zeros((META, feat), bf16)
        out[s, cap:, :cap] = notes[:, s * cap : (s + 1) * cap]


def unpack_kernel(sections, cap, mp_ref, arrived, embed, x0_out, x1_out, notes_out, place_out, count_out):
    slots = sections * cap
    m = mp_ref[0]
    rows = jnp.concatenate([arrived[s, :cap, :] for s in range(sections)], axis=0)
    notes = jnp.concatenate([arrived[s, cap:, :cap] for s in range(sections)], axis=1)
    live = notes[META - 1 : META, :].astype(f32)
    before = (iota((slots, slots), 0) < iota((slots, slots), 1)).astype(bf16)
    rank = jnp.dot(jnp.broadcast_to(live, (8, slots)).astype(bf16), before, preferred_element_type=f32)
    rank = rank[:1].astype(jnp.int32)
    served = jnp.sum(live).astype(jnp.int32)
    fits = [(served * den <= slots * num).astype(jnp.int32) for num, den in SHARES]
    count_out[0] = sum(fits[1:], 0)
    group = slots // 4
    for (num, den), fit in zip(SHARES[1:], fits[1:]):
        group = group + fit * (slots * num // den // 4 - group)
    block = sum((rank >= j * group).astype(jnp.int32) for j in range(1, 4))
    place = jnp.where(live > 0, (block ^ m) * group + (rank - block * group), -1)
    size = slots
    select = (iota((size, slots), 0) == place).astype(bf16)
    x0 = jnp.dot(select, rows, preferred_element_type=f32)
    mine = nt_dot(select, notes)
    own = (mine[:, 0:1] * DIGIT + mine[:, 1:2]).astype(jnp.int32)
    other = (mine[:, 2:3] * DIGIT + mine[:, 3:4]).astype(jnp.int32)
    columns = iota((size, embed.shape[0]), 1)
    effect = jnp.where(columns == own, 1.0, 0.0) + jnp.where(columns == other, 0.5, 0.0)
    moved = jnp.dot(effect.astype(bf16), embed[...], preferred_element_type=f32)
    x0_out[...] = x0.astype(bf16)
    x1_out[...] = (0.8 * x0 + moved).astype(bf16)
    notes_out[...] = mine[: size // 4]
    place_out[...] = place


def hidden_kernel(size, tile, mp_ref, own, px, py, da, db, w_in, hidden, mine, x_full, scale):
    feat = own.shape[1]
    group = size // 4
    width, inner = w_in.shape
    m = mp_ref[0]
    total = jnp.zeros((size, 1), f32)
    for k in range(4):
        parts = []
        for j in range(4):
            b = j ^ k
            if k == 3:
                src = da if b < 2 else db
                parts.append(src[(b % 2) * group : (b % 2 + 1) * group, :])
            else:
                src = (own, px, py)[k]
                parts.append(src[b * group : (b + 1) * group, :])
        chunk = jnp.concatenate(parts, axis=0)
        x_full[:, pl.ds(pl.multiple_of((m ^ k) * feat, feat), feat)] = chunk
        wide = chunk.astype(f32)
        total = total + jnp.sum(wide * wide, axis=1, keepdims=True)
    scale[...] = lax.rsqrt(total / width + norm_eps)
    mine[...] = x_full[:group, :]

    @pl.loop(0, inner // tile)
    def _(t):
        cols = pl.ds(pl.multiple_of(t * tile, tile), tile)
        z = jnp.dot(x_full[...], w_in[:, cols], preferred_element_type=f32)
        hidden[:, cols] = jax.nn.gelu(z * scale[...]).astype(bf16)


def near_kernel(size, tile, mp_ref, own, px, py, w_in, *rest):
    *ends, chunks, w_here, arrived, halved = rest
    halves = []
    if len(ends) == 6:
        first, second, z, square, left, right = ends
        h = left.shape[0]
        halves.append(pltpu.make_async_copy(first.at[pl.ds(0, h)], left, halved.at[0]))
        halves.append(pltpu.make_async_copy(second.at[pl.ds(h, h)], right, halved.at[1]))
    else:
        z, square = ends
    feat = own.shape[1]
    group = size // 4
    m = mp_ref[0]

    def fetch(k, t):
        rows = pl.ds(pl.multiple_of((m ^ k) * feat, feat), feat)
        cols = pl.ds(pl.multiple_of(t * tile, tile), tile)
        return pltpu.make_async_copy(w_in.at[rows, cols], w_here.at[k, :, cols], arrived.at[k, t])

    tiles = w_in.shape[1] // tile
    for t in range(tiles):
        for k in range(3):
            fetch(k, t).start()
    for copy in halves:
        copy.start()
    total = jnp.zeros((size, 1), f32)
    for k, src in enumerate((own, px, py)):
        for j in range(4):
            chunks[k, j * group : (j + 1) * group, :] = src[(j ^ k) * group : ((j ^ k) + 1) * group, :]
        wide = chunks[k].astype(f32)
        total = total + jnp.sum(wide * wide, axis=1, keepdims=True)
    square[...] = total

    @pl.loop(0, tiles)
    def _(t):
        cols = pl.ds(pl.multiple_of(t * tile, tile), tile)
        for k in range(3):
            fetch(k, t).wait()
        z[:, cols] = sum(jnp.dot(chunks[k], w_here[k, :, cols], preferred_element_type=f32) for k in range(3))

    for copy in halves:
        copy.wait()


def far_kernel(size, tile, mp_ref, z, square, own, px, py, da, db, w_in, hidden, mine, chunk, scale):
    feat = own.shape[1]
    group = size // 4
    width = 4 * feat
    m = mp_ref[0]
    for j in range(4):
        src = db if j < 2 else da
        chunk[j * group : (j + 1) * group, :] = src[((j ^ 3) % 2) * group : ((j ^ 3) % 2 + 1) * group, :]
    wide = chunk[...].astype(f32)
    total = square[...] + jnp.sum(wide * wide, axis=1, keepdims=True)
    scale[...] = lax.rsqrt(total / width + norm_eps)
    rows = [pl.ds(pl.multiple_of((m ^ k) * feat, feat), feat) for k in range(4)]
    mine[:, rows[0]] = own[:group, :]
    mine[:, rows[1]] = px[group : 2 * group, :]
    mine[:, rows[2]] = py[2 * group : 3 * group, :]
    mine[:, rows[3]] = chunk[:group, :]

    @pl.loop(0, w_in.shape[1] // tile)
    def _(t):
        cols = pl.ds(pl.multiple_of(t * tile, tile), tile)
        total = z[:, cols] + jnp.dot(chunk[...], w_in[rows[3], cols], preferred_element_type=f32)
        hidden[:, cols] = jax.nn.gelu(total * scale[...]).astype(bf16)


def part_kernel(size, tile, hidden, w_out, send_a, send_b, keep_a, keep_b):
    group = size // 4
    half = w_out.shape[1] // 2
    for side in range(2):
        keep, send, order = ((keep_a, send_a, (0, 2, 1, 3)), (keep_b, send_b, (0, 1, 2, 3)))[side]

        @pl.loop(0, half // tile)
        def _(t):
            cols = pl.ds(pl.multiple_of(t * tile, tile), tile)
            from_cols = pl.ds(pl.multiple_of(t * tile + side * half, tile), tile)
            part = jnp.dot(hidden[...], w_out[:, from_cols], preferred_element_type=f32).astype(bf16)
            for i, j in enumerate(order):
                ref = keep if i < 2 else send
                ref[(i % 2) * group : (i % 2 + 1) * group, cols] = part[j * group : (j + 1) * group]


def fold_kernel(keep_a, got_a, keep_b, got_b, out_a, out_b):
    out_a[...] = (keep_a[...].astype(f32) + got_a[...].astype(f32)).astype(bf16)
    out_b[...] = (keep_b[...].astype(f32) + got_b[...].astype(f32)).astype(bf16)


def score_kernel(sections, cap, step_idx, mp_ref, mine, keep_a, got_a, last_a, keep_b, got_b, last_b, h0, h1, h2, h3_top, h3_bottom, notes, place, *rest):
    earlier, out = rest[:-1], rest[-1]
    group, width = mine.shape
    half = width // 2
    m = mp_ref[0]
    wide = lambda ref: ref[...].astype(f32)
    sum_a = keep_a[:group].astype(f32) + got_a[:group].astype(f32) + wide(last_a)
    sum_b = keep_b[:group].astype(f32) + got_b[:group].astype(f32) + wide(last_b)
    x = wide(mine)
    ha = x[:, :half] + sum_a
    hb = x[:, half:] + sum_b
    square = jnp.sum(ha * ha, axis=1, keepdims=True) + jnp.sum(hb * hb, axis=1, keepdims=True)
    scale = lax.rsqrt(square / width + norm_eps)
    na = (ha * scale).astype(bf16)
    nb = (hb * scale).astype(bf16)
    c = 4 * step_idx
    chosen = (notes[:, c : c + 1] * DIGIT + notes[:, c + 1 : c + 2]).astype(jnp.int32)
    logits = []
    heads = ((h0[:half], h0[half:]), (h1[:half], h1[half:]), (h2[:half], h2[half:]), (h3_top[...], h3_bottom[...]))
    for top, bottom in heads:
        logits.append(
            jnp.dot(na, top, preferred_element_type=f32) + jnp.dot(nb, bottom, preferred_element_type=f32)
        )
    peak = functools.reduce(jnp.maximum, [jnp.max(v, axis=1, keepdims=True) for v in logits])
    total = jnp.zeros((group, 1), f32)
    picked = jnp.zeros((group, 1), f32)
    for k, v in enumerate(logits):
        columns = iota(v.shape, 1) + (m ^ k) * v.shape[1]
        total = total + jnp.sum(jnp.exp(v - peak), axis=1, keepdims=True)
        picked = picked + jnp.sum(jnp.where(columns == chosen, v, 0.0), axis=1, keepdims=True)
    logp = picked - peak - jnp.log(total)
    slots = sections * cap
    spread = jnp.where(iota((group, slots), 0) == place[...], logp, 0.0)
    spread = jnp.sum(spread, axis=0, keepdims=True)
    if not earlier:
        for s in range(sections):
            out[s : s + 1, :] = spread[:, s * cap : (s + 1) * cap]
        return
    for s in range(sections):
        row = jnp.concatenate([earlier[0][s : s + 1, :], spread[:, s * cap : (s + 1) * cap]], axis=1)
        out[4 * s : 4 * s + 4, :] = jnp.broadcast_to(row, (4, 2 * cap))


def return_kernel(sections, cap, agents, got, out):
    own_row = owners_row(agents)
    rows = own_row.shape[1]
    dest = own_row * cap + slots_row(own_row)
    pick = (iota((sections * cap, rows), 0) == dest).astype(f32)
    sums = [jnp.sum(got[4 * a : 4 * a + 4, :], axis=0, keepdims=True) for a in range(sections)]
    steps = [jnp.concatenate([v[:, t * cap : (t + 1) * cap] for v in sums], axis=1) for t in range(STEPS)]
    steps = jnp.concatenate(steps + [jnp.zeros((8 - STEPS, sections * cap), f32)], axis=0)
    found = jnp.dot(steps, pick, precision=lax.Precision.HIGHEST, preferred_element_type=f32)
    for t in range(STEPS):
        for p in range(2):
            out[t, p : p + 1, :] = found[t : t + 1, p * rows // 2 : (p + 1) * rows // 2]


def call(kernel, outs, cost=None, grant=VMEM, **kw):
    return pl.pallas_call(
        kernel,
        out_shape=outs,
        compiler_params=pltpu.CompilerParams(vmem_limit_bytes=grant),
        cost_estimate=cost,
        **kw,
    )


def shape(*dims, dtype=bf16):
    return jax.ShapeDtypeStruct(dims, dtype)


SMEM_SPEC = pl.BlockSpec(memory_space=pltpu.SMEM)
HBM_SPEC = pl.BlockSpec(memory_space=pltpu.HBM)
VMEM_SPEC = pl.BlockSpec(memory_space=pltpu.VMEM)


def serve_rows(sections, cap, size, over_x, over_y, m, x0, x1, notes, place, w_in, w_out, *heads):
    feat = x0.shape[1]
    width = w_in.shape[0]
    inner = w_in.shape[1]
    group = size // 4

    h = size // 2
    flops = 2 * size * width * inner

    def near(v):
        return over_x(v), over_y(v)

    def far(from_x, from_y):
        return over_y(from_x[:h]), over_x(from_y[h:])

    def to_hidden(x, near_x, far_x):
        return call(
            functools.partial(hidden_kernel, size, TILE),
            (shape(size, inner), shape(group, width)),
            cost=pl.CostEstimate(flops=flops, bytes_accessed=2 * width * inner, transcendentals=size * inner),
            in_specs=[SMEM_SPEC] + [VMEM_SPEC] * 6,
            scratch_shapes=[pltpu.VMEM((size, width), bf16), pltpu.VMEM((size, 1), f32)],
        )(m, x, *near_x, *far_x, w_in)

    def to_near(x, near_x, *wholes):
        halves = tuple(shape(v.shape[0] // 2, v.shape[1]) for v in wholes)
        any_spec = pl.BlockSpec(memory_space=pl.ANY)
        return call(
            functools.partial(near_kernel, size, TILE),
            (shape(size, inner, dtype=f32), shape(size, 1, dtype=f32)) + halves,
            cost=pl.CostEstimate(flops=3 * flops // 4, bytes_accessed=2 * width * inner, transcendentals=0),
            in_specs=[SMEM_SPEC] + [VMEM_SPEC] * 3 + [any_spec] * (1 + len(wholes)),
            out_specs=(VMEM_SPEC,) * 2 + (any_spec,) * len(halves),
            scratch_shapes=[
                pltpu.VMEM((3, size, feat), bf16),
                pltpu.VMEM((3, feat, inner), bf16),
                pltpu.SemaphoreType.DMA((3, inner // TILE)),
                pltpu.SemaphoreType.DMA((2,)),
            ],
        )(m, x, *near_x, w_in, *wholes)

    def finish_hidden(z, square, x, near_x, far_x):
        return call(
            functools.partial(far_kernel, size, TILE),
            (shape(size, inner), shape(group, width)),
            cost=pl.CostEstimate(flops=flops // 4, bytes_accessed=width * inner // 2, transcendentals=size * inner),
            in_specs=[SMEM_SPEC] + [VMEM_SPEC] * 8,
            scratch_shapes=[pltpu.VMEM((size, feat), bf16), pltpu.VMEM((size, 1), f32)],
        )(m, z, square, x, *near_x, *far_x, w_in)

    def to_parts(hidden):
        return call(
            functools.partial(part_kernel, size, TILE),
            (shape(h, width // 2),) * 4,
            cost=pl.CostEstimate(flops=flops, bytes_accessed=2 * width * inner, transcendentals=0),
        )(hidden, w_out)

    def fold(keep_a, got_a, keep_b, got_b):
        second = pl.BlockSpec((group, width // 2), lambda i: (1, 0))
        whole = pl.BlockSpec((group, width // 2), lambda i: (0, 0))
        return call(
            fold_kernel,
            (shape(group, width // 2),) * 2,
            grid=(1,),
            in_specs=[second] * 4,
            out_specs=(whole,) * 2,
        )(keep_a, got_a, keep_b, got_b)

    def score(step_idx, pieces, *earlier):
        return call(
            functools.partial(score_kernel, sections, cap, step_idx),
            shape(4 * sections, 2 * cap, dtype=f32) if earlier else shape(sections, cap, dtype=f32),
            in_specs=[SMEM_SPEC] + [VMEM_SPEC] * (14 + len(earlier)),
        )(m, *pieces, head_own, head_x, head_y, *head_far, notes, place, *earlier)

    x0, x1, notes = x0[:size], x1[:size], notes[:group]
    near0 = near(x0)
    far0 = far(*near0)
    head_own, head_x, head_y = heads
    z0, square0, left, right = to_near(x0, near0, head_x, head_y)
    x1, *near0 = lax.optimization_barrier((x1, *near0))
    near1 = near(x1)
    z0, left, right, *near1 = lax.optimization_barrier((z0, left, right, *near1))
    head_far = over_y(left), over_x(right)
    hidden0, mine0 = finish_hidden(z0, square0, x0, near0, far0)
    far1 = far(*near1)
    send_a0, send_b0, keep_a0, keep_b0 = to_parts(hidden0)
    got_a0, got_b0 = over_x(send_a0), over_y(send_b0)
    hidden1, mine1 = to_hidden(x1, near1, far1)
    fold_a0, fold_b0 = fold(keep_a0, got_a0, keep_b0, got_b0)
    last_a0, last_b0 = over_y(fold_a0), over_x(fold_b0)
    send_a1, send_b1, keep_a1, keep_b1 = to_parts(hidden1)
    got_a1, got_b1 = over_x(send_a1), over_y(send_b1)
    got_a1, *head_far = lax.optimization_barrier((got_a1, *head_far))
    fold_a1, fold_b1 = fold(keep_a1, got_a1, keep_b1, got_b1)
    last_a1, last_b1 = over_y(fold_a1), over_x(fold_b1)
    first = score(0, (mine0, keep_a0, got_a0, last_a0, keep_b0, got_b0, last_b0))
    return score(1, (mine1, keep_a1, got_a1, last_a1, keep_b1, got_b1, last_b1), first)


def plane_plan(matches, actions, state, embed, w_in, w_out, head):
    sections = lax.axis_size("section")
    games, _, feat = state.shape
    cap = 4 * games // sections
    rows = 2 * games
    slots = sections * cap
    width = 4 * feat
    m = lax.axis_index("mp").astype(jnp.int32).reshape(1)
    over_x = lambda v: lax.ppermute(v, "mp", [(i, i ^ 1) for i in range(4)])
    over_y = lambda v: lax.ppermute(v, "mp", [(i, i ^ 2) for i in range(4)])

    agents = matches.T
    acts = actions.transpose(0, 2, 1)

    head_own = head[0]
    head_x, head_y = over_x(head_own), over_y(head_own)
    others = (head_x, head_y)

    packed = call(
        functools.partial(pack_kernel, sections, cap),
        shape(sections, cap + META, feat),
        grant=60 * 1024 * 1024,
        in_specs=[HBM_SPEC] * 3,
        scratch_shapes=[
            pltpu.VMEM(agents.shape, jnp.int32),
            pltpu.VMEM(acts.shape, jnp.int32),
            pltpu.VMEM(state.shape, f32),
            pltpu.SemaphoreType.DMA((3,)),
        ],
    )(agents, acts, state)
    arrived = lax.all_to_all(packed, "section", split_axis=0, concat_axis=0, tiled=True)
    x0, x1, notes_c, place, count = call(
        functools.partial(unpack_kernel, sections, cap),
        (
            shape(slots, feat), shape(slots, feat), shape(slots // 4, META, dtype=f32),
            shape(1, slots, dtype=jnp.int32), shape(1, dtype=jnp.int32),
        ),
        in_specs=[SMEM_SPEC, VMEM_SPEC, VMEM_SPEC],
        out_specs=(VMEM_SPEC,) * 4 + (SMEM_SPEC,),
    )(m, arrived, embed)

    x0, *others = lax.optimization_barrier((x0,) + others)
    heads = (head_own, *others)

    branches = [
        functools.partial(serve_rows, sections, cap, slots * num // den, over_x, over_y) for num, den in SHARES
    ]
    sent = lax.switch(count[0], branches, m, x0, x1, notes_c, place, w_in[0, 0], w_out[0, 0], *heads)
    back = lax.all_to_all(sent, ("section", "mp"), split_axis=0, concat_axis=0, tiled=True)
    logp = call(functools.partial(return_kernel, sections, cap), shape(STEPS, 2, games, dtype=f32))(agents, back)
    return logp.transpose(0, 2, 1)


def general_plan(matches, actions, state, embed, w_in, w_out, head):
    sections = lax.axis_size("section")
    game_count = matches.shape[0]
    feat_width = state.shape[2]
    slot_cap = 4 * game_count // sections
    served = sections * slot_cap
    owners = matches.reshape(-1)
    onehot = (owners[:, None] == jnp.arange(sections, dtype=jnp.int32)[None, :]).astype(jnp.int32)
    slot_of = jnp.sum((jnp.cumsum(onehot, axis=0) - onehot) * onehot, axis=1)
    action_width = head.shape[2]
    columns = lax.axis_index("mp") * action_width + jnp.arange(action_width, dtype=jnp.int32)
    current = state
    results = []
    for step_idx in range(STEPS):
        observed = current.astype(bf16).reshape(2 * game_count, feat_width)
        outgoing = jnp.zeros((sections, slot_cap, feat_width), bf16).at[owners, slot_of].set(observed)
        arrived = lax.all_to_all(outgoing, "section", split_axis=0, concat_axis=0, tiled=True)
        inputs = lax.all_gather(arrived.reshape(served, feat_width), "mp", axis=1, tiled=True)
        normed = rms_round(inputs)
        hidden = jax.nn.gelu(jnp.dot(normed, w_in[0, 0], preferred_element_type=f32)).astype(bf16)
        partial_value = jnp.dot(hidden, w_out[0, 0], preferred_element_type=f32)
        summed = inputs.astype(f32) + lax.psum(partial_value.astype(bf16), "mp").astype(f32)
        logits = jnp.dot(rms_round(summed), head[0], preferred_element_type=f32)
        returned = lax.all_to_all(
            logits.reshape(sections, slot_cap, action_width).astype(bf16),
            "section",
            split_axis=0,
            concat_axis=0,
            tiled=True,
        ).astype(f32)
        row_logits = returned[owners, slot_of]
        row_peak = lax.pmax(jnp.max(row_logits, axis=1), "mp")
        chosen = actions[step_idx].reshape(-1)
        local_total = jnp.sum(jnp.exp(row_logits - row_peak[:, None]), axis=1)
        local_pick = jnp.sum(jnp.where(columns[None, :] == chosen[:, None], row_logits, 0.0), axis=1)
        row_total, picked = lax.psum((local_total, local_pick), "mp")
        results.append((picked - row_peak - jnp.log(row_total)).reshape(game_count, 2))
        picked_rows = jnp.take(embed, actions[step_idx], axis=0).astype(f32)
        current = 0.8 * current + picked_rows + 0.5 * picked_rows[:, ::-1, :]
    return jnp.stack(results)


def solution(mesh):
    return jax.shard_map(
        plane_plan if mesh.shape["mp"] == 4 else general_plan,
        mesh=mesh,
        in_specs=(
            P("section", None),
            P(None, "section", None),
            P("section", None, "mp"),
            P(None, "mp"),
            P("section", None, None, "mp"),
            P("section", None, "mp", None),
            P("section", None, "mp"),
        ),
        out_specs=P(None, "section", None),
        check_vma=False,
    )
```

```python
import functools

import jax
import jax.numpy as jnp
from jax import lax
from jax.experimental import pallas as pl
from jax.experimental.pallas import tpu as pltpu
from jax.sharding import PartitionSpec as P

STEPS = 2
META = 8
DIGIT = 32
SHARES = ((1, 1), (5, 8), (3, 8))
TILE = 512
VMEM = 20 * 1024 * 1024

norm_eps = 1e-06
f32 = jnp.float32
bf16 = jnp.bfloat16


def rms_round(source):
    widened = source.astype(f32)
    scale = lax.rsqrt(jnp.mean(widened * widened, axis=-1, keepdims=True) + norm_eps)
    return (widened * scale).astype(bf16)


def iota(shape, dim):
    return lax.broadcasted_iota(jnp.int32, shape, dim)


def nt_dot(left, right):
    return lax.dot_general(left, right, (((1,), (1,)), ((), ())), preferred_element_type=f32)


def slots_row(own_row):
    rows = own_row.shape[1]
    lower, upper = iota((rows, rows), 0), iota((rows, rows), 1)
    own_col = jnp.sum(jnp.where(lower == upper, own_row, 0), axis=1, keepdims=True)
    earlier = (own_col == own_row) & (lower < upper)
    return jnp.sum(earlier.astype(jnp.int32), axis=0, keepdims=True)


def owners_row(pair):
    return jnp.concatenate([pair[0:1, :], pair[1:2, :]], axis=1)


def pack_kernel(sections, cap, agents, acts, state, out, agents_here, acts_here, state_here, done):
    copies = [
        pltpu.make_async_copy(far, here, done.at[i])
        for i, (far, here) in enumerate(((agents, agents_here), (acts, acts_here), (state, state_here)))
    ]
    for copy in copies:
        copy.start()
    games, _, feat = state_here.shape
    rows = 2 * games
    copies[0].wait()
    own_row = owners_row(agents_here)
    dest = own_row * cap + slots_row(own_row)
    select = (iota((sections * cap, rows), 0) == dest).astype(bf16)
    copies[1].wait()
    first, second = (acts_here[0, p : p + 1, :] for p in range(2))
    mine0 = jnp.concatenate([first, second], axis=1)
    other0 = jnp.concatenate([second, first], axis=1)
    mine1 = jnp.concatenate([acts_here[1, 0:1, :], acts_here[1, 1:2, :]], axis=1)
    digits = [v for a in (mine0, other0, mine1) for v in (a // DIGIT, a % DIGIT)]
    meta = jnp.concatenate(digits + [jnp.zeros_like(mine0), jnp.ones_like(mine0)], axis=0).astype(f32).astype(bf16)
    notes = nt_dot(meta, select).astype(bf16)
    copies[2].wait()
    packed = jnp.dot(select[:, :games], state_here[:, 0, :].astype(bf16), preferred_element_type=f32)
    packed = packed + jnp.dot(select[:, games:], state_here[:, 1, :].astype(bf16), preferred_element_type=f32)
    packed = packed.astype(bf16)
    for s in range(sections):
        out[s, :cap, :] = packed[s * cap : (s + 1) * cap]
        out[s, cap:, :] = jnp.zeros((META, feat), bf16)
        out[s, cap:, :cap] = notes[:, s * cap : (s + 1) * cap]


def unpack_kernel(sections, cap, mp_ref, arrived, embed, x0_out, x1_out, notes_out, place_out, count_out):
    slots = sections * cap
    m = mp_ref[0]
    rows = jnp.concatenate([arrived[s, :cap, :] for s in range(sections)], axis=0)
    notes = jnp.concatenate([arrived[s, cap:, :cap] for s in range(sections)], axis=1)
    live = notes[META - 1 : META, :].astype(f32)
    before = (iota((slots, slots), 0) < iota((slots, slots), 1)).astype(bf16)
    rank = jnp.dot(jnp.broadcast_to(live, (8, slots)).astype(bf16), before, preferred_element_type=f32)
    rank = rank[:1].astype(jnp.int32)
    served = jnp.sum(live).astype(jnp.int32)
    fits = [(served * den <= slots * num).astype(jnp.int32) for num, den in SHARES]
    count_out[0] = sum(fits[1:], 0)
    group = slots // 4
    for (num, den), fit in zip(SHARES[1:], fits[1:]):
        group = group + fit * (slots * num // den // 4 - group)
    block = sum((rank >= j * group).astype(jnp.int32) for j in range(1, 4))
    place = jnp.where(live > 0, (block ^ m) * group + (rank - block * group), -1)
    size = slots
    select = (iota((size, slots), 0) == place).astype(bf16)
    x0 = jnp.dot(select, rows, preferred_element_type=f32)
    mine = nt_dot(select, notes)
    own = (mine[:, 0:1] * DIGIT + mine[:, 1:2]).astype(jnp.int32)
    other = (mine[:, 2:3] * DIGIT + mine[:, 3:4]).astype(jnp.int32)
    columns = iota((size, embed.shape[0]), 1)
    effect = jnp.where(columns == own, 1.0, 0.0) + jnp.where(columns == other, 0.5, 0.0)
    moved = jnp.dot(effect.astype(bf16), embed[...], preferred_element_type=f32)
    x0_out[...] = x0.astype(bf16)
    x1_out[...] = (0.8 * x0 + moved).astype(bf16)
    notes_out[...] = mine[: size // 4]
    place_out[...] = place


def hidden_kernel(size, tile, mp_ref, own, px, py, da, db, w_in, hidden, mine, x_full, scale):
    feat = own.shape[1]
    group = size // 4
    width, inner = w_in.shape
    m = mp_ref[0]
    total = jnp.zeros((size, 1), f32)
    for k in range(4):
        parts = []
        for j in range(4):
            b = j ^ k
            if k == 3:
                src = da if b < 2 else db
                parts.append(src[(b % 2) * group : (b % 2 + 1) * group, :])
            else:
                src = (own, px, py)[k]
                parts.append(src[b * group : (b + 1) * group, :])
        chunk = jnp.concatenate(parts, axis=0)
        x_full[:, pl.ds(pl.multiple_of((m ^ k) * feat, feat), feat)] = chunk
        wide = chunk.astype(f32)
        total = total + jnp.sum(wide * wide, axis=1, keepdims=True)
    scale[...] = lax.rsqrt(total / width + norm_eps)
    mine[...] = x_full[:group, :]

    @pl.loop(0, inner // tile)
    def _(t):
        cols = pl.ds(pl.multiple_of(t * tile, tile), tile)
        z = jnp.dot(x_full[...], w_in[:, cols], preferred_element_type=f32)
        hidden[:, cols] = jax.nn.gelu(z * scale[...]).astype(bf16)


def near_kernel(size, tile, mp_ref, own, px, py, w_in, *rest):
    *ends, chunks, w_here, arrived, halved = rest
    halves = []
    if len(ends) == 6:
        first, second, z, square, left, right = ends
        h = left.shape[0]
        halves.append(pltpu.make_async_copy(first.at[pl.ds(0, h)], left, halved.at[0]))
        halves.append(pltpu.make_async_copy(second.at[pl.ds(h, h)], right, halved.at[1]))
    else:
        z, square = ends
    feat = own.shape[1]
    group = size // 4
    m = mp_ref[0]

    def fetch(k, t):
        rows = pl.ds(pl.multiple_of((m ^ k) * feat, feat), feat)
        cols = pl.ds(pl.multiple_of(t * tile, tile), tile)
        return pltpu.make_async_copy(w_in.at[rows, cols], w_here.at[k, :, cols], arrived.at[k, t])

    tiles = w_in.shape[1] // tile
    for t in range(tiles):
        for k in range(3):
            fetch(k, t).start()
    for copy in halves:
        copy.start()
    total = jnp.zeros((size, 1), f32)
    for k, src in enumerate((own, px, py)):
        for j in range(4):
            chunks[k, j * group : (j + 1) * group, :] = src[(j ^ k) * group : ((j ^ k) + 1) * group, :]
        wide = chunks[k].astype(f32)
        total = total + jnp.sum(wide * wide, axis=1, keepdims=True)
    square[...] = total

    @pl.loop(0, tiles)
    def _(t):
        cols = pl.ds(pl.multiple_of(t * tile, tile), tile)
        for k in range(3):
            fetch(k, t).wait()
        z[:, cols] = sum(jnp.dot(chunks[k], w_here[k, :, cols], preferred_element_type=f32) for k in range(3))

    for copy in halves:
        copy.wait()


def far_kernel(size, tile, mp_ref, z, square, own, px, py, da, db, w_in, hidden, mine, chunk, scale):
    feat = own.shape[1]
    group = size // 4
    width = 4 * feat
    m = mp_ref[0]
    for j in range(4):
        src = db if j < 2 else da
        chunk[j * group : (j + 1) * group, :] = src[((j ^ 3) % 2) * group : ((j ^ 3) % 2 + 1) * group, :]
    wide = chunk[...].astype(f32)
    total = square[...] + jnp.sum(wide * wide, axis=1, keepdims=True)
    scale[...] = lax.rsqrt(total / width + norm_eps)
    rows = [pl.ds(pl.multiple_of((m ^ k) * feat, feat), feat) for k in range(4)]
    mine[:, rows[0]] = own[:group, :]
    mine[:, rows[1]] = px[group : 2 * group, :]
    mine[:, rows[2]] = py[2 * group : 3 * group, :]
    mine[:, rows[3]] = chunk[:group, :]

    @pl.loop(0, w_in.shape[1] // tile)
    def _(t):
        cols = pl.ds(pl.multiple_of(t * tile, tile), tile)
        total = z[:, cols] + jnp.dot(chunk[...], w_in[rows[3], cols], preferred_element_type=f32)
        hidden[:, cols] = jax.nn.gelu(total * scale[...]).astype(bf16)


def part_kernel(size, tile, hidden, w_out, send_a, send_b, keep_a, keep_b):
    group = size // 4
    half = w_out.shape[1] // 2
    for side in range(2):
        keep, send, order = ((keep_a, send_a, (0, 2, 1, 3)), (keep_b, send_b, (0, 1, 2, 3)))[side]

        @pl.loop(0, half // tile)
        def _(t):
            cols = pl.ds(pl.multiple_of(t * tile, tile), tile)
            from_cols = pl.ds(pl.multiple_of(t * tile + side * half, tile), tile)
            part = jnp.dot(hidden[...], w_out[:, from_cols], preferred_element_type=f32).astype(bf16)
            for i, j in enumerate(order):
                ref = keep if i < 2 else send
                ref[(i % 2) * group : (i % 2 + 1) * group, cols] = part[j * group : (j + 1) * group]


def fold_kernel(keep, got, out):
    out[...] = (keep[...].astype(f32) + got[...].astype(f32)).astype(bf16)


def score_kernel(sections, cap, step_idx, mp_ref, mine, keep_a, got_a, last_a, keep_b, got_b, last_b, h0, h1, h2, h3_top, h3_bottom, notes, place, *rest):
    earlier, out = rest[:-1], rest[-1]
    group, width = mine.shape
    half = width // 2
    m = mp_ref[0]
    wide = lambda ref: ref[...].astype(f32)
    sum_a = keep_a[:group].astype(f32) + got_a[:group].astype(f32) + wide(last_a)
    sum_b = keep_b[:group].astype(f32) + got_b[:group].astype(f32) + wide(last_b)
    x = wide(mine)
    ha = x[:, :half] + sum_a
    hb = x[:, half:] + sum_b
    square = jnp.sum(ha * ha, axis=1, keepdims=True) + jnp.sum(hb * hb, axis=1, keepdims=True)
    scale = lax.rsqrt(square / width + norm_eps)
    na = (ha * scale).astype(bf16)
    nb = (hb * scale).astype(bf16)
    c = 4 * step_idx
    chosen = (notes[:, c : c + 1] * DIGIT + notes[:, c + 1 : c + 2]).astype(jnp.int32)
    logits = []
    heads = ((h0[:half], h0[half:]), (h1[:half], h1[half:]), (h2[:half], h2[half:]), (h3_top[...], h3_bottom[...]))
    for top, bottom in heads:
        logits.append(
            jnp.dot(na, top, preferred_element_type=f32) + jnp.dot(nb, bottom, preferred_element_type=f32)
        )
    peak = functools.reduce(jnp.maximum, [jnp.max(v, axis=1, keepdims=True) for v in logits])
    total = jnp.zeros((group, 1), f32)
    picked = jnp.zeros((group, 1), f32)
    for k, v in enumerate(logits):
        columns = iota(v.shape, 1) + (m ^ k) * v.shape[1]
        total = total + jnp.sum(jnp.exp(v - peak), axis=1, keepdims=True)
        picked = picked + jnp.sum(jnp.where(columns == chosen, v, 0.0), axis=1, keepdims=True)
    logp = picked - peak - jnp.log(total)
    slots = sections * cap
    spread = jnp.where(iota((group, slots), 0) == place[...], logp, 0.0)
    spread = jnp.sum(spread, axis=0, keepdims=True)
    if not earlier:
        for s in range(sections):
            out[s : s + 1, :] = spread[:, s * cap : (s + 1) * cap]
        return
    for s in range(sections):
        row = jnp.concatenate([earlier[0][s : s + 1, :], spread[:, s * cap : (s + 1) * cap]], axis=1)
        out[4 * s : 4 * s + 4, :] = jnp.broadcast_to(row, (4, 2 * cap))


def return_kernel(sections, cap, agents, got, out):
    own_row = owners_row(agents)
    rows = own_row.shape[1]
    dest = own_row * cap + slots_row(own_row)
    pick = (iota((sections * cap, rows), 0) == dest).astype(f32)
    sums = [jnp.sum(got[4 * a : 4 * a + 4, :], axis=0, keepdims=True) for a in range(sections)]
    steps = [jnp.concatenate([v[:, t * cap : (t + 1) * cap] for v in sums], axis=1) for t in range(STEPS)]
    steps = jnp.concatenate(steps + [jnp.zeros((8 - STEPS, sections * cap), f32)], axis=0)
    found = jnp.dot(steps, pick, precision=lax.Precision.HIGHEST, preferred_element_type=f32)
    for t in range(STEPS):
        for p in range(2):
            out[t, p : p + 1, :] = found[t : t + 1, p * rows // 2 : (p + 1) * rows // 2]


def call(kernel, outs, cost=None, grant=VMEM, **kw):
    return pl.pallas_call(
        kernel,
        out_shape=outs,
        compiler_params=pltpu.CompilerParams(vmem_limit_bytes=grant),
        cost_estimate=cost,
        **kw,
    )


def shape(*dims, dtype=bf16):
    return jax.ShapeDtypeStruct(dims, dtype)


SMEM_SPEC = pl.BlockSpec(memory_space=pltpu.SMEM)
HBM_SPEC = pl.BlockSpec(memory_space=pltpu.HBM)
VMEM_SPEC = pl.BlockSpec(memory_space=pltpu.VMEM)


def serve_rows(sections, cap, size, over_x, over_y, m, x0, x1, notes, place, w_in, w_out, *heads):
    feat = x0.shape[1]
    width = w_in.shape[0]
    inner = w_in.shape[1]
    group = size // 4

    h = size // 2
    flops = 2 * size * width * inner

    def near(v):
        return over_x(v), over_y(v)

    def far(from_x, from_y):
        return over_y(from_x[:h]), over_x(from_y[h:])

    def to_hidden(x, near_x, far_x):
        return call(
            functools.partial(hidden_kernel, size, TILE),
            (shape(size, inner), shape(group, width)),
            cost=pl.CostEstimate(flops=flops, bytes_accessed=2 * width * inner, transcendentals=size * inner),
            in_specs=[SMEM_SPEC] + [VMEM_SPEC] * 6,
            scratch_shapes=[pltpu.VMEM((size, width), bf16), pltpu.VMEM((size, 1), f32)],
        )(m, x, *near_x, *far_x, w_in)

    def to_near(x, near_x, *wholes):
        halves = tuple(shape(v.shape[0] // 2, v.shape[1]) for v in wholes)
        any_spec = pl.BlockSpec(memory_space=pl.ANY)
        return call(
            functools.partial(near_kernel, size, TILE),
            (shape(size, inner, dtype=f32), shape(size, 1, dtype=f32)) + halves,
            cost=pl.CostEstimate(flops=3 * flops // 4, bytes_accessed=2 * width * inner, transcendentals=0),
            in_specs=[SMEM_SPEC] + [VMEM_SPEC] * 3 + [any_spec] * (1 + len(wholes)),
            out_specs=(VMEM_SPEC,) * 2 + (any_spec,) * len(halves),
            scratch_shapes=[
                pltpu.VMEM((3, size, feat), bf16),
                pltpu.VMEM((3, feat, inner), bf16),
                pltpu.SemaphoreType.DMA((3, inner // TILE)),
                pltpu.SemaphoreType.DMA((2,)),
            ],
        )(m, x, *near_x, w_in, *wholes)

    def finish_hidden(z, square, x, near_x, far_x):
        return call(
            functools.partial(far_kernel, size, TILE),
            (shape(size, inner), shape(group, width)),
            cost=pl.CostEstimate(flops=flops // 4, bytes_accessed=width * inner // 2, transcendentals=size * inner),
            in_specs=[SMEM_SPEC] + [VMEM_SPEC] * 8,
            scratch_shapes=[pltpu.VMEM((size, feat), bf16), pltpu.VMEM((size, 1), f32)],
        )(m, z, square, x, *near_x, *far_x, w_in)

    def to_parts(hidden):
        return call(
            functools.partial(part_kernel, size, TILE),
            (shape(h, width // 2),) * 4,
            cost=pl.CostEstimate(flops=flops, bytes_accessed=2 * width * inner, transcendentals=0),
        )(hidden, w_out)

    def fold(keep, got):
        second = pl.BlockSpec((group, width // 2), lambda i: (1, 0))
        return call(
            fold_kernel,
            shape(group, width // 2),
            grid=(1,),
            in_specs=[second] * 2,
            out_specs=pl.BlockSpec((group, width // 2), lambda i: (0, 0)),
        )(keep, got)

    def score(step_idx, pieces, *earlier):
        return call(
            functools.partial(score_kernel, sections, cap, step_idx),
            shape(4 * sections, 2 * cap, dtype=f32) if earlier else shape(sections, cap, dtype=f32),
            in_specs=[SMEM_SPEC] + [VMEM_SPEC] * (14 + len(earlier)),
        )(m, *pieces, head_own, head_x, head_y, *head_far, notes, place, *earlier)

    x0, x1, notes = x0[:size], x1[:size], notes[:group]
    near0 = near(x0)
    far0 = far(*near0)
    head_own, head_x, head_y = heads
    z0, square0, left, right = to_near(x0, near0, head_x, head_y)
    x1, *near0 = lax.optimization_barrier((x1, *near0))
    near1 = near(x1)
    z0, left, right, *near1 = lax.optimization_barrier((z0, left, right, *near1))
    head_far = over_y(left), over_x(right)
    hidden0, mine0 = finish_hidden(z0, square0, x0, near0, far0)
    far1 = far(*near1)
    send_a0, send_b0, keep_a0, keep_b0 = to_parts(hidden0)
    got_a0, got_b0 = over_x(send_a0), over_y(send_b0)
    hidden1, mine1 = to_hidden(x1, near1, far1)
    fold_a0, fold_b0 = fold(keep_a0, got_a0), fold(keep_b0, got_b0)
    last_a0, last_b0 = over_y(fold_a0), over_x(fold_b0)
    send_a1, send_b1, keep_a1, keep_b1 = to_parts(hidden1)
    got_a1, got_b1 = over_x(send_a1), over_y(send_b1)
    got_a1, *head_far = lax.optimization_barrier((got_a1, *head_far))
    fold_a1, fold_b1 = fold(keep_a1, got_a1), fold(keep_b1, got_b1)
    last_a1, last_b1 = over_y(fold_a1), over_x(fold_b1)
    first = score(0, (mine0, keep_a0, got_a0, last_a0, keep_b0, got_b0, last_b0))
    return score(1, (mine1, keep_a1, got_a1, last_a1, keep_b1, got_b1, last_b1), first)


def plane_plan(matches, actions, state, embed, w_in, w_out, head):
    sections = lax.axis_size("section")
    games, _, feat = state.shape
    cap = 4 * games // sections
    rows = 2 * games
    slots = sections * cap
    width = 4 * feat
    m = lax.axis_index("mp").astype(jnp.int32).reshape(1)
    over_x = lambda v: lax.ppermute(v, "mp", [(i, i ^ 1) for i in range(4)])
    over_y = lambda v: lax.ppermute(v, "mp", [(i, i ^ 2) for i in range(4)])

    agents = matches.T
    acts = actions.transpose(0, 2, 1)

    head_own = head[0]
    head_x, head_y = over_x(head_own), over_y(head_own)
    others = (head_x, head_y)

    packed = call(
        functools.partial(pack_kernel, sections, cap),
        shape(sections, cap + META, feat),
        grant=60 * 1024 * 1024,
        in_specs=[HBM_SPEC] * 3,
        scratch_shapes=[
            pltpu.VMEM(agents.shape, jnp.int32),
            pltpu.VMEM(acts.shape, jnp.int32),
            pltpu.VMEM(state.shape, f32),
            pltpu.SemaphoreType.DMA((3,)),
        ],
    )(agents, acts, state)
    arrived = lax.all_to_all(packed, "section", split_axis=0, concat_axis=0, tiled=True)
    x0, x1, notes_c, place, count = call(
        functools.partial(unpack_kernel, sections, cap),
        (
            shape(slots, feat), shape(slots, feat), shape(slots // 4, META, dtype=f32),
            shape(1, slots, dtype=jnp.int32), shape(1, dtype=jnp.int32),
        ),
        in_specs=[SMEM_SPEC, VMEM_SPEC, VMEM_SPEC],
        out_specs=(VMEM_SPEC,) * 4 + (SMEM_SPEC,),
    )(m, arrived, embed)

    x0, *others = lax.optimization_barrier((x0,) + others)
    heads = (head_own, *others)

    branches = [
        functools.partial(serve_rows, sections, cap, slots * num // den, over_x, over_y) for num, den in SHARES
    ]
    sent = lax.switch(count[0], branches, m, x0, x1, notes_c, place, w_in[0, 0], w_out[0, 0], *heads)
    back = lax.all_to_all(sent, ("section", "mp"), split_axis=0, concat_axis=0, tiled=True)
    logp = call(functools.partial(return_kernel, sections, cap), shape(STEPS, 2, games, dtype=f32))(agents, back)
    return logp.transpose(0, 2, 1)


def general_plan(matches, actions, state, embed, w_in, w_out, head):
    sections = lax.axis_size("section")
    game_count = matches.shape[0]
    feat_width = state.shape[2]
    slot_cap = 4 * game_count // sections
    served = sections * slot_cap
    owners = matches.reshape(-1)
    onehot = (owners[:, None] == jnp.arange(sections, dtype=jnp.int32)[None, :]).astype(jnp.int32)
    slot_of = jnp.sum((jnp.cumsum(onehot, axis=0) - onehot) * onehot, axis=1)
    action_width = head.shape[2]
    columns = lax.axis_index("mp") * action_width + jnp.arange(action_width, dtype=jnp.int32)
    current = state
    results = []
    for step_idx in range(STEPS):
        observed = current.astype(bf16).reshape(2 * game_count, feat_width)
        outgoing = jnp.zeros((sections, slot_cap, feat_width), bf16).at[owners, slot_of].set(observed)
        arrived = lax.all_to_all(outgoing, "section", split_axis=0, concat_axis=0, tiled=True)
        inputs = lax.all_gather(arrived.reshape(served, feat_width), "mp", axis=1, tiled=True)
        normed = rms_round(inputs)
        hidden = jax.nn.gelu(jnp.dot(normed, w_in[0, 0], preferred_element_type=f32)).astype(bf16)
        partial_value = jnp.dot(hidden, w_out[0, 0], preferred_element_type=f32)
        summed = inputs.astype(f32) + lax.psum(partial_value.astype(bf16), "mp").astype(f32)
        logits = jnp.dot(rms_round(summed), head[0], preferred_element_type=f32)
        returned = lax.all_to_all(
            logits.reshape(sections, slot_cap, action_width).astype(bf16),
            "section",
            split_axis=0,
            concat_axis=0,
            tiled=True,
        ).astype(f32)
        row_logits = returned[owners, slot_of]
        row_peak = lax.pmax(jnp.max(row_logits, axis=1), "mp")
        chosen = actions[step_idx].reshape(-1)
        local_total = jnp.sum(jnp.exp(row_logits - row_peak[:, None]), axis=1)
        local_pick = jnp.sum(jnp.where(columns[None, :] == chosen[:, None], row_logits, 0.0), axis=1)
        row_total, picked = lax.psum((local_total, local_pick), "mp")
        results.append((picked - row_peak - jnp.log(row_total)).reshape(game_count, 2))
        picked_rows = jnp.take(embed, actions[step_idx], axis=0).astype(f32)
        current = 0.8 * current + picked_rows + 0.5 * picked_rows[:, ::-1, :]
    return jnp.stack(results)


def solution(mesh):
    return jax.shard_map(
        plane_plan if mesh.shape["mp"] == 4 else general_plan,
        mesh=mesh,
        in_specs=(
            P("section", None),
            P(None, "section", None),
            P("section", None, "mp"),
            P(None, "mp"),
            P("section", None, None, "mp"),
            P("section", None, "mp", None),
            P("section", None, "mp"),
        ),
        out_specs=P(None, "section", None),
        check_vma=False,
    )
```
